256 devices in a mesh: ctx: 32 (over z, x_hi, core), head: 8 (over y, x_lo).
Axes of the slice: x: 4 (x_hi: 2, x_lo: 2; x = x_hi * 2 + x_lo), y: 4, z: 8, core: 2. Of those that a mesh axis runs over, the one named last changes fastest.
Arguments:
- queries: bfloat16 [4096, 6144], P('ctx', 'head'), may hold values from -6 to 6
- key_states: bfloat16 [4096, 1024], P('ctx', 'head'), may hold values from -8 to 8
- value_states: bfloat16 [4096, 1024], P('ctx', 'head'), may hold values from -6 to 6
- out_grad: bfloat16 [4096, 6144], P('ctx', 'head'), may hold values from -6 to 6
- norm_gain: float32 [6144], P('head'), may hold values from 0.1 to 1.9
- mask_kind: int32 [8], replicated, may hold values from 0 to 1
- range_start: int32 [8], replicated, may hold values from 0 to 7, as said below
- placement: int32 [8], replicated, may hold values from 0 to 7, each once
Outputs:
- attn_out: bfloat16 [4096, 6144], P('ctx', 'head')
- d_queries: bfloat16 [4096, 6144], P('ctx', 'head')
- d_keys: bfloat16 [4096, 1024], P('ctx', 'head')
- d_values: bfloat16 [4096, 1024], P('ctx', 'head')
The draws below stay inside these ranges and needn't reach their ends.
Inputs may be any that keep to these rules, and one draw needn't show every extreme that they name: range_start[i] <= i for every span i; the last span sees no earlier span. `placement`: every span number appears in exactly one slot.
All inputs are finite; a program needn't handle non-finite values.
Results may differ from the reference program's by a relative error of at most 0.04.
Values may be sent and summed in bfloat16 or wider, within the bound.
No kernel may reach another device: no remote copies, remote signals or barrier semaphores. Data moves between devices by JAX's collectives and lax.ppermute only.
A program may use at most 64 MiB of HBM per device.

```python
import math
import jax
import jax.numpy as jnp
from jax import lax

HEAD_DIM = 128
GROUP = 6
KV_HEADS = 8
HEADS = 48
SPAN_LEN = 512
TOKENS = 4096
SPANS = 8


def draw_queries(key, part):
    key = jax.random.fold_in(key, 11)
    noise_key = jax.random.fold_in(key, 0)
    head_ids = jnp.arange(HEADS, dtype=jnp.float32)
    sample = jax.random.normal(noise_key, (TOKENS, HEADS, HEAD_DIM), jnp.float32)
    head_scale = jnp.sqrt(1.0 + 3.0 * head_ids / max(HEADS - 1, 1))
    sample = sample * head_scale[None, :, None]
    return jnp.clip(sample, -6.0, 6.0).reshape(TOKENS, HEADS * HEAD_DIM).astype(jnp.bfloat16)


def draw_key_states(key, part):
    key = jax.random.fold_in(key, 17)
    noise_key = jax.random.fold_in(key, 0)
    sample = jax.random.normal(noise_key, (TOKENS, KV_HEADS, HEAD_DIM), jnp.float32)
    return jnp.clip(sample, -8.0, 8.0).reshape(TOKENS, KV_HEADS * HEAD_DIM).astype(jnp.bfloat16)


def draw_range_start(key, part):
    key = jax.random.fold_in(key, 23)
    span_ids = jnp.arange(SPANS, dtype=jnp.int32)
    reach = jax.random.randint(key, (SPANS,), 0, SPANS, dtype=jnp.int32)
    reach = jnp.where(span_ids == SPANS - 1, 0, reach)
    return jnp.maximum(span_ids - reach, 0)


def plant(entries, key, smallest, top_value):
    longest = entries.shape.index(max(entries.shape))
    spots = []
    for shift in (0, 1):
        where = [jax.random.randint(jax.random.fold_in(key, axis), (), 0, length) for axis, length in enumerate(entries.shape)]
        where[longest] = (where[longest] + shift) % entries.shape[longest]
        spots.append(tuple(where))
    return entries.at[spots[0]].set(smallest).at[spots[1]].set(top_value)


def level_of(own_key, dims, pieces, least, high):
    def one(dim, blocks):
        draws = jax.random.uniform(jax.random.fold_in(jax.random.fold_in(own_key, 6), dim), (blocks,), jnp.float32, least / len(pieces), high / len(pieces))
        return jnp.repeat(jnp.exp(draws), dims[dim] // blocks).reshape((-1,) + (1,) * (len(dims) - dim - 1))

    level = one(*pieces[0])
    for cut in pieces[1:]:
        level = level * one(*cut)
    return level


def noise(own_key, shape, spread, limit, shards=(), kind=jnp.bfloat16):
    values = jax.random.normal(own_key, shape, jnp.float32) * spread
    if len(shards) > 0:
        values = level_of(own_key, shape, shards, -0.22, 0.18) * values
    return jnp.clip(values, min=-limit, max=limit).astype(kind)


def setup_inputs(seed: int = 0) -> dict:
    keys = jax.random.split(jax.random.key(seed), 9)
    return {
        "queries": draw_queries(jax.random.fold_in(keys[8], 71), 0),
        "key_states": draw_key_states(jax.random.fold_in(keys[8], 71), 0),
        "value_states": noise(keys[2], (TOKENS, KV_HEADS * HEAD_DIM), 2.0, 6.0, ((0, 32), (1, 8))),
        "out_grad": noise(keys[3], (TOKENS, HEADS * HEAD_DIM), 1.0, 6.0, ((0, 32), (1, 8))),
        "norm_gain": jnp.clip(1.0 + 0.18 * jax.random.normal(keys[4], (HEADS * HEAD_DIM,), jnp.float32), 0.1, 1.9),
        "mask_kind": plant(jax.random.randint(keys[5], (SPANS,), 0, 2), jax.random.fold_in(keys[5], 1), 0, 1).astype(jnp.int32),
        "range_start": draw_range_start(jax.random.fold_in(keys[8], 71), 0),
        "placement": jax.random.permutation(keys[7], SPANS).astype(jnp.int32),
    }


NEG = -1e+30
EPS = 1e-06

def dot_rows(left_side, right_side):
    return lax.dot_general(left_side, right_side, (((1,), (1,)), ((), ())), preferred_element_type=jnp.float32)

def dot_cols(left_side, right_side):
    return lax.dot_general(left_side, right_side, (((0,), (0,)), ((), ())), preferred_element_type=jnp.float32)

def reference(queries, key_states, value_states, out_grad, norm_gain, mask_kind, range_start, placement):
    full_width = HEADS * HEAD_DIM
    group_width = GROUP * HEAD_DIM
    inv_sqrt = 1.0 / math.sqrt(HEAD_DIM)
    query_f = queries.astype(jnp.float32)
    inv_rms = lax.rsqrt(lax.optimization_barrier(jnp.sum(query_f * query_f, axis=1)) / full_width + EPS)
    normed = (query_f * inv_rms[:, None] * norm_gain[None, :]).astype(jnp.bfloat16)
    block_len = min(512, TOKENS)
    n_blocks = TOKENS // block_len
    all_rows = jnp.arange(TOKENS, dtype=jnp.int32)
    row_span = placement[all_rows // SPAN_LEN]
    row_pos = all_rows % SPAN_LEN
    row_lower = range_start[row_span]
    row_causal = mask_kind[row_span]

    def per_group(group_idx):
        q_group = lax.dynamic_slice_in_dim(normed, group_idx * group_width, group_width, 1)
        g_group = lax.dynamic_slice_in_dim(out_grad, group_idx * group_width, group_width, 1)
        key_group = lax.dynamic_slice_in_dim(key_states, group_idx * HEAD_DIM, HEAD_DIM, 1)
        value_group = lax.dynamic_slice_in_dim(value_states, group_idx * HEAD_DIM, HEAD_DIM, 1)

        def one_block(grads, block_idx):
            d_key_acc, d_value_acc = grads
            first_row = block_idx * block_len
            rows_q = lax.dynamic_slice_in_dim(q_group, first_row, block_len, 0).reshape(block_len * GROUP, HEAD_DIM)
            rows_g = lax.dynamic_slice_in_dim(g_group, first_row, block_len, 0).reshape(block_len * GROUP, HEAD_DIM)
            q_span = lax.dynamic_slice_in_dim(row_span, first_row, block_len, 0)
            q_pos = lax.dynamic_slice_in_dim(row_pos, first_row, block_len, 0)
            q_lower = lax.dynamic_slice_in_dim(row_lower, first_row, block_len, 0)
            q_causal = lax.dynamic_slice_in_dim(row_causal, first_row, block_len, 0)
            before = (q_lower[:, None] <= row_span[None, :]) & (row_span[None, :] < q_span[:, None])
            same_span = (row_span[None, :] == q_span[:, None]) & ((q_causal[:, None] == 0) | (row_pos[None, :] <= q_pos[:, None]))
            allowed = (before | same_span)[:, None, :]
            scores = dot_rows(rows_q, key_group).reshape(block_len, GROUP, TOKENS) * inv_sqrt
            row_max = lax.optimization_barrier(jnp.max(jnp.where(allowed, scores, NEG), axis=2))
            weights = jnp.exp(jnp.where(allowed, scores - row_max[..., None], NEG))
            row_sum = lax.optimization_barrier(jnp.sum(weights, axis=2))
            mixed = jnp.dot(weights.astype(jnp.bfloat16).reshape(block_len * GROUP, TOKENS), value_group, preferred_element_type=jnp.float32).reshape(block_len, GROUP, HEAD_DIM)
            out_block = (mixed / row_sum[..., None]).astype(jnp.bfloat16)
            log_sum = row_max + jnp.log(row_sum)
            out_delta = lax.optimization_barrier(jnp.sum(rows_g.astype(jnp.float32).reshape(block_len, GROUP, HEAD_DIM) * out_block.astype(jnp.float32), axis=2))
            attn_prob = jnp.exp(jnp.where(allowed, scores - log_sum[..., None], NEG))
            d_prob = dot_rows(rows_g, value_group).reshape(block_len, GROUP, TOKENS)
            dscore = (attn_prob * (d_prob - out_delta[..., None]) * inv_sqrt).astype(jnp.bfloat16).reshape(block_len * GROUP, TOKENS)
            d_query_block = jnp.dot(dscore, key_group, preferred_element_type=jnp.float32)
            d_key_acc = d_key_acc + dot_cols(dscore, rows_q)
            prob_bf = attn_prob.astype(jnp.bfloat16).reshape(block_len * GROUP, TOKENS)
            d_value_acc = d_value_acc + dot_cols(prob_bf, rows_g)
            return ((d_key_acc, d_value_acc), (out_block.reshape(block_len, group_width), d_query_block.reshape(block_len, group_width)))
        zero_grad = jnp.zeros((TOKENS, HEAD_DIM), jnp.float32)
        grads_out, rows_out = lax.scan(one_block, (zero_grad, zero_grad), jnp.arange(n_blocks, dtype=jnp.int32))
        out_rows, dq_rows = rows_out
        return (out_rows.reshape(TOKENS, group_width), dq_rows.reshape(TOKENS, group_width), grads_out[0].astype(jnp.bfloat16), grads_out[1].astype(jnp.bfloat16))
    out_all, dq_all, dk_all, dv_all = lax.map(per_group, jnp.arange(KV_HEADS, dtype=jnp.int32))
    attn_out = jnp.transpose(out_all, (1, 0, 2)).reshape(TOKENS, full_width)
    d_normed = jnp.transpose(dq_all, (1, 0, 2)).reshape(TOKENS, full_width)
    d_keys = jnp.transpose(dk_all, (1, 0, 2)).reshape(TOKENS, KV_HEADS * HEAD_DIM)
    d_values = jnp.transpose(dv_all, (1, 0, 2)).reshape(TOKENS, KV_HEADS * HEAD_DIM)
    d_queries = d_normed.astype(jnp.bfloat16)
    return (attn_out, d_queries, d_keys, d_values)
```

```python
import functools
import math

import jax
import jax.numpy as jnp
from jax import lax
from jax.experimental import pallas as pl
from jax.experimental.pallas import tpu as pltpu
from jax.sharding import Mesh
from jax.sharding import PartitionSpec as P

NEG = -1e30
EPS = 1e-06
SPAN_DEVS = 4
LOG2E = 1.4426950408889634
LN2 = 0.6931471805599453

CTX = ("z", "xh", "core")
HEAD = ("y", "xl")


def dot_rows(left_side, right_side):
    return lax.dot_general(
        left_side, right_side, (((1,), (1,)), ((), ())), preferred_element_type=jnp.float32
    )


def dot_cols(left_side, right_side):
    return lax.dot_general(
        left_side, right_side, (((0,), (0,)), ((), ())), preferred_element_type=jnp.float32
    )


def dot(left_side, right_side):
    return jnp.dot(left_side, right_side, preferred_element_type=jnp.float32)


def attend(
    plan, queries, out_grad, square_sum, gain, kv, attn_out, d_queries, dkv,
    q_rows, g_rows, score, prob, ds_rows, row_max, row_sum, acc,
    *, tok, heads, dim, span_len, spans, width,
):
    count = plan[0]
    inv_sqrt = 1.0 / math.sqrt(dim)
    lanes = [slice(h * dim, (h + 1) * dim) for h in range(heads)]
    rows = [slice(h * tok, (h + 1) * tok) for h in range(heads)]
    inv_rms = lax.rsqrt(square_sum[...] / width + EPS) * (inv_sqrt * LOG2E)
    for h in range(heads):
        scaled = queries[:, lanes[h]].astype(jnp.float32) * inv_rms * gain[:, lanes[h]]
        q_rows[rows[h], :] = scaled.astype(jnp.bfloat16)
    row_max[...] = jnp.full_like(row_max, NEG)
    row_sum[...] = jnp.zeros_like(row_sum)
    acc[...] = jnp.zeros_like(acc)

    def lane_tiles(x):
        return [x[:, j * 128 : (j + 1) * 128] for j in range(x.shape[1] // 128)]

    def score_block(i, masked):
        slot = plan[3 + i]
        keys = kv[slot, :, :dim]
        if masked:
            q_pos = plan[2] + lax.broadcasted_iota(jnp.int32, (tok, span_len), 0)
            k_pos = lax.broadcasted_iota(jnp.int32, (tok, span_len), 1)
            allowed = (k_pos <= q_pos) | (plan[1] == 0)
        for h in range(heads):
            s = dot_rows(q_rows[rows[h], :], keys)
            if masked:
                s = jnp.where(allowed, s, NEG)
            score[i, rows[h], :] = s
            row_max[rows[h], :] = functools.reduce(
                jnp.maximum, lane_tiles(s), row_max[rows[h], :]
            )

    @pl.loop(0, count - 1)
    def _(i):
        score_block(i, False)

    score_block(count - 1, True)
    for h in range(heads):
        top = jnp.max(row_max[rows[h], :], axis=1, keepdims=True)
        row_max[rows[h], :] = jnp.broadcast_to(top, (tok, 128))

    @pl.loop(0, count)
    def _(i):
        slot = plan[3 + i]
        values = kv[slot, :, dim:]
        for h in range(heads):
            top = row_max[rows[h], :]
            tiles = [jnp.exp2(t - top) for t in lane_tiles(score[i, rows[h], :])]
            row_sum[rows[h], :] += functools.reduce(jnp.add, tiles)
            p = jnp.concatenate(tiles, axis=1).astype(jnp.bfloat16)
            prob[i, rows[h], :] = p
            acc[rows[h], :] += dot(p, values)

    for h in range(heads):
        inv_sum = 1.0 / jnp.sum(row_sum[rows[h], :], axis=1, keepdims=True)
        out = (acc[rows[h], :] * inv_sum).astype(jnp.bfloat16)
        attn_out[:, lanes[h]] = out
        grad = out_grad[:, lanes[h]].astype(jnp.float32) * inv_sum
        g_rows[rows[h], :] = grad.astype(jnp.bfloat16)
        delta = jnp.sum(grad * out.astype(jnp.float32), axis=1, keepdims=True)
        row_sum[rows[h], :] = jnp.broadcast_to(delta, (tok, 128))
    acc[...] = jnp.zeros_like(acc)

    @pl.loop(0, spans)
    def _(slot):
        @pl.when(plan[3 + spans + slot] == 0)
        def _():
            dkv[slot] = jnp.zeros(dkv.shape[1:], dkv.dtype)

    @pl.loop(0, count)
    def _(i):
        slot = plan[3 + i]
        keys = kv[slot, :, :dim]
        values = kv[slot, :, dim:]
        for h in range(heads):
            delta = row_sum[rows[h], :]
            d_prob = dot_rows(g_rows[rows[h], :], values)
            p = prob[i, rows[h], :].astype(jnp.float32)
            tiles = [a * (b - delta) for a, b in zip(lane_tiles(p), lane_tiles(d_prob))]
            ds = jnp.concatenate(tiles, axis=1).astype(jnp.bfloat16)
            ds_rows[rows[h], :] = ds
            acc[rows[h], :] += dot(ds, keys)
        d_keys = dot_cols(ds_rows[...], q_rows[...]) * LN2
        d_values = dot_cols(prob[i], g_rows[...])
        dkv[slot, :, :dim] = d_keys.astype(jnp.bfloat16)
        dkv[slot, :, dim:] = d_values.astype(jnp.bfloat16)

    for h in range(heads):
        d_queries[:, lanes[h]] = (acc[rows[h], :] * inv_sqrt).astype(jnp.bfloat16)


def attend_call(plan, queries, out_grad, square_sum, gain, kv, width):
    tok, local = queries.shape
    spans, span_len, both = kv.shape
    dim = both // 2
    heads = local // dim
    kernel = functools.partial(
        attend, tok=tok, heads=heads, dim=dim, span_len=span_len, spans=spans, width=width
    )
    vmem = pl.BlockSpec(memory_space=pltpu.VMEM)
    n_rows = heads * tok
    return pl.pallas_call(
        kernel,
        out_shape=(
            jax.ShapeDtypeStruct((tok, local), jnp.bfloat16),
            jax.ShapeDtypeStruct((tok, local), jnp.bfloat16),
            jax.ShapeDtypeStruct(kv.shape, jnp.bfloat16),
        ),
        in_specs=[pl.BlockSpec(memory_space=pltpu.SMEM)] + [vmem] * 5,
        out_specs=[vmem] * 3,
        scratch_shapes=[
            pltpu.VMEM((n_rows, dim), jnp.bfloat16),
            pltpu.VMEM((n_rows, dim), jnp.bfloat16),
            pltpu.VMEM((spans, n_rows, span_len), jnp.float32),
            pltpu.VMEM((spans, n_rows, span_len), jnp.bfloat16),
            pltpu.VMEM((n_rows, span_len), jnp.bfloat16),
            pltpu.VMEM((n_rows, 128), jnp.float32),
            pltpu.VMEM((n_rows, 128), jnp.float32),
            pltpu.VMEM((n_rows, dim), jnp.float32),
        ],
        compiler_params=pltpu.CompilerParams(vmem_limit_bytes=40 * 2**20),
        name="attend",
    )(plan, queries, out_grad, square_sum, gain, kv)


def make_plan(mask_kind, range_start, placement, rank, tok):
    spans = placement.shape[0]
    own_slot = rank // SPAN_DEVS
    slot_ids = jnp.arange(spans, dtype=jnp.int32)
    own_span = jnp.sum(jnp.where(slot_ids == own_slot, placement, 0))
    lower = jnp.sum(jnp.where(slot_ids == own_span, range_start, 0))
    causal = jnp.sum(jnp.where(slot_ids == own_span, mask_kind, 0))
    seen = ((lower <= placement) & (placement <= own_span)).astype(jnp.int32)
    block = placement - lower
    order = jnp.sum(
        jnp.where((block[None, :] == slot_ids[:, None]) & (seen[None, :] == 1), slot_ids, 0), axis=1
    )
    head = jnp.stack([own_span - lower + 1, causal, (rank % SPAN_DEVS) * tok])
    return jnp.concatenate([head, order, seen]).astype(jnp.int32)


def shards(
    queries, key_states, value_states, out_grad, norm_gain, mask_kind, range_start, placement
):
    rank = lax.axis_index(CTX)
    tok, local = queries.shape
    spans = placement.shape[0]
    dim = key_states.shape[1]
    n_heads = lax.axis_size(HEAD)
    query_f = queries.astype(jnp.float32)
    partial = jnp.sum(query_f * query_f, axis=1)
    parts = lax.all_to_all(
        jnp.broadcast_to(partial[None, None, :], (n_heads, 1, tok)), HEAD, 0, 0
    )
    square_sum = jnp.sum(parts, axis=0).reshape(tok, 1)

    n_far = lax.axis_size(("z", "xh"))
    kv_own = jnp.concatenate([key_states, value_states], axis=1)
    core = lax.axis_index("core")
    kv_mine = lax.all_to_all(
        jnp.broadcast_to(kv_own[None], (n_far,) + kv_own.shape), ("z", "xh"), 0, 0
    )
    kv_other = lax.ppermute(kv_mine, "core", [(0, 1), (1, 0)])
    kv_all = jnp.where(
        core == 0,
        jnp.stack([kv_mine, kv_other], axis=1),
        jnp.stack([kv_other, kv_mine], axis=1),
    ).reshape(spans, SPAN_DEVS * tok, 2 * dim)

    plan = make_plan(mask_kind, range_start, placement, rank, tok)
    attn_out, d_queries, dkv = attend_call(
        plan, queries, out_grad, square_sum, norm_gain[None, :], kv_all, local * n_heads
    )

    dkv = dkv.reshape(n_far, 2, tok, 2 * dim)
    keep = jnp.where(core == 0, dkv[:, 0], dkv[:, 1])
    give = jnp.where(core == 0, dkv[:, 1], dkv[:, 0])
    got = lax.ppermute(give, "core", [(0, 1), (1, 0)])
    chip = (keep.astype(jnp.float32) + got.astype(jnp.float32)).astype(jnp.bfloat16)
    pieces = lax.all_to_all(chip, ("z", "xh"), 0, 0)
    total = jnp.sum(pieces.astype(jnp.float32), axis=0).astype(jnp.bfloat16)
    return (attn_out, d_queries, total[:, :dim], total[:, dim:])


def solution(mesh):
    fine = Mesh(mesh.devices.reshape(8, 2, 2, 4, 2), ("z", "xh", "core", "y", "xl"))
    rows = P(CTX, HEAD)
    in_specs = (rows, rows, rows, rows, P(HEAD), P(), P(), P())
    out_specs = (rows, rows, rows, rows)
    return jax.shard_map(shards, mesh=fine, in_specs=in_specs, out_specs=out_specs, check_vma=False)
```

```python
import functools
import math

import jax
import jax.numpy as jnp
from jax import lax
from jax.experimental import pallas as pl
from jax.experimental.pallas import tpu as pltpu
from jax.sharding import Mesh
from jax.sharding import PartitionSpec as P

NEG = -1e30
EPS = 1e-06
LOG2E = 1.4426950408889634
LN2 = 0.6931471805599453
LANES = 128
STATS = 3

CTX = ("z", "xh", "core")
HEAD = ("y", "xl")
SWAP = [(0, 1), (1, 0)]
VMEM_LIMIT = 44 * 2**20


def dot_rows(left_side, right_side):
    return lax.dot_general(
        left_side, right_side, (((1,), (1,)), ((), ())), preferred_element_type=jnp.float32
    )


def dot_cols(left_side, right_side):
    return lax.dot_general(
        left_side, right_side, (((0,), (0,)), ((), ())), preferred_element_type=jnp.float32
    )


def dot(left_side, right_side):
    return jnp.dot(left_side, right_side, preferred_element_type=jnp.float32)


def lane_tiles(x):
    return [x[:, j : j + LANES] for j in range(0, x.shape[1], LANES)]


def lane_sum(x):
    return jnp.sum(x, axis=1, keepdims=True)


def visible_slots(placement, range_start, place, order):
    own_span = placement[place[0]]
    lower = range_start[own_span]

    @pl.loop(0, placement.shape[0])
    def _(slot):
        span = placement[slot]

        @pl.when((lower <= span) & (span <= own_span))
        def _():
            order[span - lower] = slot

    return own_span - lower + 1, own_span


def forward(
    place, mask_kind, range_start, placement, q_own, q_mate, g_own, g_mate, kv_mine, kv_mate,
    prob_out, acc, stats,
    order, q_rows, score, prob, row_max, row_sum, sems,
    *, tok, heads, dim, group,
):
    count, own_span = visible_slots(placement, range_start, place, order)
    half = heads * tok
    keys_n = 2 * tok
    for h in range(heads):
        q_rows[h * tok : (h + 1) * tok, :] = q_own[:, h * dim : (h + 1) * dim]
        q_rows[half + h * tok : half + (h + 1) * tok, :] = q_mate[:, h * dim : (h + 1) * dim]
    row_max[...] = jnp.full_like(row_max, NEG)
    row_sum[...] = jnp.zeros_like(row_sum)
    acc[...] = jnp.zeros_like(acc)
    chunks = [slice(r, r + group) for r in range(0, 2 * half, group)]

    def score_block(i, masked):
        slot = order[i]
        keys = jnp.concatenate([kv_mine[slot, :, :dim], kv_mate[slot, :, :dim]], axis=0)
        if masked:
            free = mask_kind[own_span] == 0
            q_t = lax.broadcasted_iota(jnp.int32, (group, keys_n), 0) % tok
            k_t = lax.broadcasted_iota(jnp.int32, (group, keys_n), 1)
            core = place[2]
            k_pos = place[1] * keys_n + jnp.where(
                k_t < tok, core * tok + k_t, (1 - core) * tok + k_t - tok
            )
        for c in chunks:
            s = dot_rows(q_rows[c, :], keys)
            if masked:
                q_xh = place[1] if c.start < half else 1 - place[1]
                q_pos = (q_xh * 2 + core) * tok + q_t
                s = jnp.where((k_pos <= q_pos) | free, s, NEG)
            score[i, c, :] = s
            row_max[c, :] = functools.reduce(jnp.maximum, lane_tiles(s), row_max[c, :])

    @pl.loop(0, count - 1)
    def _(i):
        score_block(i, False)

    score_block(count - 1, True)
    for c in chunks:
        top = jnp.max(row_max[c, :], axis=1, keepdims=True)
        row_max[c, :] = jnp.broadcast_to(top, (group, LANES))

    @pl.loop(0, count)
    def _(i):
        slot = order[i]
        values = jnp.concatenate([kv_mine[slot, :, dim:], kv_mate[slot, :, dim:]], axis=0)
        for c in chunks:
            top = row_max[c, :]
            tiles = [jnp.exp2(t - top) for t in lane_tiles(score[i, c, :])]
            row_sum[c, :] += functools.reduce(jnp.add, tiles)
            p = jnp.concatenate(tiles, axis=1).astype(jnp.bfloat16)
            prob[i, c, :] = p
            acc[c, :] += dot(p, values)
        pltpu.make_async_copy(prob.at[i], prob_out.at[i], sems.at[i]).start()

    lane = lax.broadcasted_iota(jnp.int32, (tok, LANES), 1)
    table = jnp.zeros((tok, LANES), jnp.float32)
    for j in range(2 * heads):
        r = slice(j * tok, (j + 1) * tok)
        grads = g_own if j < heads else g_mate
        h = j % heads
        grad = grads[:, h * dim : (h + 1) * dim].astype(jnp.float32)
        table = jnp.where(lane == STATS * j, row_max[r, :], table)
        table = jnp.where(lane == STATS * j + 1, lane_sum(row_sum[r, :]), table)
        table = jnp.where(lane == STATS * j + 2, lane_sum(grad * acc[r, :]), table)
    stats[...] = jnp.transpose(table)[: stats.shape[0], :]

    @pl.loop(0, count)
    def _(i):
        pltpu.make_async_copy(prob.at[i], prob_out.at[i], sems.at[i]).wait()


def backward(
    place, range_start, placement, stats_own, stats_mate, prob_in, acc_in,
    q_own, q_mate, g_own, g_mate, kv_mine, kv_mate,
    mix_keep, mix_give, dkv_keep, dkv_give,
    order, q_rows, g_rows, prob, ds_rows, delta_rows, acc, sems,
    *, tok, heads, dim, group,
):
    count, _ = visible_slots(placement, range_start, place, order)

    @pl.loop(0, count)
    def _(i):
        pltpu.make_async_copy(prob_in.at[i], prob.at[i], sems.at[i]).start()

    half = heads * tok
    inv_sqrt = 1.0 / math.sqrt(dim)
    pad = jnp.zeros((LANES - stats_own.shape[0], LANES), jnp.float32)
    mine = jnp.transpose(jnp.concatenate([stats_own[...], pad], axis=0))
    theirs = jnp.transpose(jnp.concatenate([stats_mate[...], pad], axis=0))
    for j in range(2 * heads):
        r = slice(j * tok, (j + 1) * tok)
        h = slice((j % heads) * dim, (j % heads + 1) * dim)
        a, b = STATS * j, STATS * ((j + heads) % (2 * heads))
        top = jnp.maximum(mine[:, a : a + 1], theirs[:, b : b + 1])
        f_mine = jnp.exp2(mine[:, a : a + 1] - top)
        f_theirs = jnp.exp2(theirs[:, b : b + 1] - top)
        total = mine[:, a + 1 : a + 2] * f_mine + theirs[:, b + 1 : b + 2] * f_theirs
        scale = f_mine / total
        delta = (mine[:, a + 2 : a + 3] * f_mine + theirs[:, b + 2 : b + 3] * f_theirs) / total
        delta_rows[r, :] = jnp.broadcast_to(delta * scale, (tok, LANES))
        queries, grads, mix = (q_own, g_own, mix_keep) if j < heads else (q_mate, g_mate, mix_give)
        q_rows[r, :] = queries[:, h]
        g_rows[r, :] = (grads[:, h].astype(jnp.float32) * scale).astype(jnp.bfloat16)
        mix[0, :, h] = (acc_in[r, :] * scale).astype(jnp.bfloat16)
    acc[...] = jnp.zeros_like(acc)
    chunks = [slice(r, r + group) for r in range(0, 2 * half, group)]

    own_span = placement[place[0]]
    lower = range_start[own_span]

    @pl.loop(0, placement.shape[0])
    def _(slot):
        @pl.when((placement[slot] < lower) | (placement[slot] > own_span))
        def _():
            dkv_keep[slot] = jnp.zeros(dkv_keep.shape[1:], dkv_keep.dtype)
            dkv_give[slot] = jnp.zeros(dkv_give.shape[1:], dkv_give.dtype)

    @pl.loop(0, count)
    def _(i):
        slot = order[i]
        keys = jnp.concatenate([kv_mine[slot, :, :dim], kv_mate[slot, :, :dim]], axis=0)
        values = jnp.concatenate([kv_mine[slot, :, dim:], kv_mate[slot, :, dim:]], axis=0)
        pltpu.make_async_copy(prob_in.at[i], prob.at[i], sems.at[i]).wait()
        for c in chunks:
            d_prob = dot_rows(g_rows[c, :], values)
            p = prob[i, c, :].astype(jnp.float32)
            delta = delta_rows[c, :]
            tiles = [x * (y - delta) for x, y in zip(lane_tiles(p), lane_tiles(d_prob))]
            ds = jnp.concatenate(tiles, axis=1).astype(jnp.bfloat16)
            ds_rows[c, :] = ds
            acc[c, :] += dot(ds, keys)
        d_keys = (dot_cols(ds_rows[...], q_rows[...]) * LN2).astype(jnp.bfloat16)
        d_values = dot_cols(prob[i], g_rows[...]).astype(jnp.bfloat16)
        dkv_keep[slot, :, :dim] = d_keys[:tok]
        dkv_keep[slot, :, dim:] = d_values[:tok]
        dkv_give[slot, :, :dim] = d_keys[tok:]
        dkv_give[slot, :, dim:] = d_values[tok:]

    for j in range(2 * heads):
        h = slice((j % heads) * dim, (j % heads + 1) * dim)
        mix = mix_keep if j < heads else mix_give
        mix[1, :, h] = (acc[j * tok : (j + 1) * tok, :] * inv_sqrt).astype(jnp.bfloat16)


SMEM_SPEC = pl.BlockSpec(memory_space=pltpu.SMEM)
VMEM_SPEC = pl.BlockSpec(memory_space=pltpu.VMEM)
ANY_SPEC = pl.BlockSpec(memory_space=pl.ANY)


def sizes_of(q_own, kv_mine):
    tok, local = q_own.shape
    spans, _, both = kv_mine.shape
    dim = both // 2
    heads = local // dim
    return spans, tok, dim, heads, 2 * heads * tok


def forward_call(place, ints, q_own, q_mate, g_own, g_mate, kv_mine, kv_mate, group=384):
    spans, tok, dim, heads, n_rows = sizes_of(q_own, kv_mine)
    stat_rows = -(-2 * heads * STATS // 16) * 16
    return pl.pallas_call(
        functools.partial(forward, tok=tok, heads=heads, dim=dim, group=group),
        out_shape=(
            jax.ShapeDtypeStruct((spans, n_rows, 2 * tok), jnp.bfloat16),
            jax.ShapeDtypeStruct((n_rows, dim), jnp.float32),
            jax.ShapeDtypeStruct((stat_rows, LANES), jnp.float32),
        ),
        in_specs=[SMEM_SPEC] * 4 + [VMEM_SPEC] * 6,
        out_specs=(ANY_SPEC, VMEM_SPEC, VMEM_SPEC),
        scratch_shapes=[
            pltpu.SMEM((spans,), jnp.int32),
            pltpu.VMEM((n_rows, dim), jnp.bfloat16),
            pltpu.VMEM((spans, n_rows, 2 * tok), jnp.float32),
            pltpu.VMEM((spans, n_rows, 2 * tok), jnp.bfloat16),
            pltpu.VMEM((n_rows, LANES), jnp.float32),
            pltpu.VMEM((n_rows, LANES), jnp.float32),
            pltpu.SemaphoreType.DMA((spans,)),
        ],
        compiler_params=pltpu.CompilerParams(vmem_limit_bytes=VMEM_LIMIT),
        name="attend_forward",
    )(place, *ints, q_own, q_mate, g_own, g_mate, kv_mine, kv_mate)


def backward_call(
    place, ints, stats_own, stats_mate, prob, acc, q_own, q_mate, g_own, g_mate, kv_mine, kv_mate,
    group=384,
):
    spans, tok, dim, heads, n_rows = sizes_of(q_own, kv_mine)
    mix = jax.ShapeDtypeStruct((2,) + q_own.shape, jnp.bfloat16)
    part = jax.ShapeDtypeStruct(kv_mine.shape, jnp.bfloat16)
    return pl.pallas_call(
        functools.partial(backward, tok=tok, heads=heads, dim=dim, group=group),
        out_shape=(mix, mix, part, part),
        in_specs=[SMEM_SPEC] * 3 + [VMEM_SPEC] * 2 + [ANY_SPEC] + [VMEM_SPEC] * 7,
        out_specs=(VMEM_SPEC,) * 4,
        scratch_shapes=[
            pltpu.SMEM((spans,), jnp.int32),
            pltpu.VMEM((n_rows, dim), jnp.bfloat16),
            pltpu.VMEM((n_rows, dim), jnp.bfloat16),
            pltpu.VMEM((spans, n_rows, 2 * tok), jnp.bfloat16),
            pltpu.VMEM((n_rows, 2 * tok), jnp.bfloat16),
            pltpu.VMEM((n_rows, LANES), jnp.float32),
            pltpu.VMEM((n_rows, dim), jnp.float32),
            pltpu.SemaphoreType.DMA((spans,)),
        ],
        compiler_params=pltpu.CompilerParams(vmem_limit_bytes=VMEM_LIMIT),
        name="attend_backward",
    )(
        place, *ints[1:], stats_own, stats_mate, prob, acc,
        q_own, q_mate, g_own, g_mate, kv_mine, kv_mate,
    )


def shards(
    queries, key_states, value_states, out_grad, norm_gain, mask_kind, range_start, placement
):
    tok, local = queries.shape
    dim = key_states.shape[1]
    n_heads = lax.axis_size(HEAD)
    n_z = lax.axis_size("z")
    place = jnp.stack([lax.axis_index("z"), lax.axis_index("xh"), lax.axis_index("core")])
    ints = (mask_kind, range_start, placement)

    kv_own = jnp.concatenate([key_states, value_states], axis=1)
    kv_mine = lax.all_to_all(jnp.broadcast_to(kv_own[None], (n_z,) + kv_own.shape), "z", 0, 0)
    g_mate = lax.ppermute(out_grad, "xh", SWAP)

    query_f = queries.astype(jnp.float32)
    partial = jnp.sum(query_f * query_f, axis=1)
    parts = lax.all_to_all(
        jnp.broadcast_to(partial[None, None, :], (n_heads, 1, tok)), HEAD, 0, 0
    )
    square_sum = jnp.sum(parts, axis=(0, 1))
    scale = lax.rsqrt(square_sum / (local * n_heads) + EPS) * (LOG2E / math.sqrt(dim))
    q_own = (query_f * scale[:, None] * norm_gain[None, :]).astype(jnp.bfloat16)
    q_mate = lax.ppermute(q_own, "xh", SWAP)
    kv_mate = lax.ppermute(kv_mine, "core", SWAP)

    prob, acc, stats = forward_call(place, ints, q_own, q_mate, out_grad, g_mate, kv_mine, kv_mate)
    stats_mate = lax.ppermute(stats, "xh", SWAP)
    mix_keep, mix_give, dkv_keep, dkv_give = backward_call(
        place, ints, stats, stats_mate, prob, acc, q_own, q_mate, out_grad, g_mate, kv_mine, kv_mate
    )
    mix_got = lax.ppermute(mix_give, "xh", SWAP)
    dkv_got = lax.ppermute(dkv_give, "core", SWAP)
    chip = (dkv_keep.astype(jnp.float32) + dkv_got.astype(jnp.float32)).astype(jnp.bfloat16)
    pieces = lax.all_to_all(chip, "z", 0, 0)
    total = jnp.sum(pieces.astype(jnp.float32), axis=0).astype(jnp.bfloat16)
    mixed = (mix_keep.astype(jnp.float32) + mix_got.astype(jnp.float32)).astype(jnp.bfloat16)
    return (mixed[0], mixed[1], total[:, :dim], total[:, dim:])


def solution(mesh):
    fine = Mesh(mesh.devices.reshape(8, 2, 2, 4, 2), ("z", "xh", "core", "y", "xl"))
    rows = P(CTX, HEAD)
    in_specs = (rows, rows, rows, rows, P(HEAD), P(), P(), P())
    out_specs = (rows, rows, rows, rows)
    return jax.shard_map(shards, mesh=fine, in_specs=in_specs, out_specs=out_specs, check_vma=False)
```

```python
import functools
import math

import jax
import jax.numpy as jnp
from jax import lax
from jax.experimental import pallas as pl
from jax.experimental.pallas import tpu as pltpu
from jax.sharding import Mesh
from jax.sharding import PartitionSpec as P

NEG = -1e30
EPS = 1e-06
LOG2E = 1.4426950408889634
LN2 = 0.6931471805599453
LANES = 128
STATS = 3

CTX = ("z", "xh", "core")
HEAD = ("y", "xl")
SWAP = [(0, 1), (1, 0)]
VMEM_LIMIT = 32 * 2**20
SMALL_LIMIT = 8 * 2**20
LONG = pl.CostEstimate(flops=2 * 10**10, bytes_accessed=2**20, transcendentals=0)
SHORT = pl.CostEstimate(flops=2**10, bytes_accessed=2**10, transcendentals=0)


def dot_rows(left_side, right_side):
    return lax.dot_general(
        left_side, right_side, (((1,), (1,)), ((), ())), preferred_element_type=jnp.float32
    )


def dot_cols(left_side, right_side):
    return lax.dot_general(
        left_side, right_side, (((0,), (0,)), ((), ())), preferred_element_type=jnp.float32
    )


def dot(left_side, right_side):
    return jnp.dot(left_side, right_side, preferred_element_type=jnp.float32)


def lane_tiles(x):
    return [x[:, j : j + LANES] for j in range(0, x.shape[1], LANES)]


def lane_sum(x):
    return jnp.sum(x, axis=1, keepdims=True)


def unpack(plan, spans):
    own_span = plan[3 + 2 * spans + plan[0]]
    lower = plan[3 + spans + own_span]
    return own_span - lower + 1, lower, own_span


def visible_slots(plan, order, spans):
    count, lower, own_span = unpack(plan, spans)

    @pl.loop(0, spans)
    def _(slot):
        span = plan[3 + 2 * spans + slot]

        @pl.when((lower <= span) & (span <= own_span))
        def _():
            order[span - lower] = slot

    return count, own_span


def columns_of(table):
    pad = jnp.zeros((LANES - table.shape[0], LANES), jnp.float32)
    return jnp.transpose(jnp.concatenate([table, pad], axis=0))


def row_squares(queries, q_mate, parts):
    for side, rows_of in enumerate((queries, q_mate)):
        wide = rows_of[...].astype(jnp.float32)
        total = functools.reduce(jnp.add, lane_tiles(wide * wide))
        parts[side : side + 1, :] = jnp.sum(jnp.transpose(total), axis=0, keepdims=True)


def prepare(queries, q_mate, out_grad, g_mate, q_raw, g_raw, *, tok, heads, dim):
    for side, (q_part, g_part) in enumerate(((queries, out_grad), (q_mate, g_mate))):
        for h in range(heads):
            first = (side * heads + h) * tok
            q_raw[first : first + tok, :] = q_part[:, h * dim : (h + 1) * dim]
            g_raw[first : first + tok, :] = g_part[:, h * dim : (h + 1) * dim]


def merge(keep, got, first, second):
    for n, out in enumerate((first, second)):
        out[...] = (keep[n].astype(jnp.float32) + got[n].astype(jnp.float32)).astype(out.dtype)


def forward(
    plan, square_sum, gain, q_raw, g_raw, kv_mine, kv_mate,
    prob, acc, stats, q_rows,
    order, score, row_max, row_sum,
    *, tok, heads, dim, group, width,
):
    spans = order.shape[0]
    half = heads * tok
    keys_n = 2 * tok
    sums = columns_of(square_sum[...])
    scale = lax.rsqrt(sums / width + EPS) * (LOG2E / math.sqrt(dim))
    for side in range(2):
        for h in range(heads):
            r = slice(side * half + h * tok, side * half + (h + 1) * tok)
            normed = q_raw[r, :].astype(jnp.float32) * scale[:, side : side + 1]
            normed = normed * gain[:, h * dim : (h + 1) * dim]
            q_rows[r, :] = normed.astype(jnp.bfloat16)
    count, own_span = visible_slots(plan, order, spans)
    row_max[...] = jnp.full_like(row_max, NEG)
    row_sum[...] = jnp.zeros_like(row_sum)
    acc[...] = jnp.zeros_like(acc)
    chunks = [slice(r, r + group) for r in range(0, 2 * half, group)]

    def score_block(i, masked):
        slot = order[i]
        keys = jnp.concatenate([kv_mine[slot, :, :dim], kv_mate[slot, :, :dim]], axis=0)
        if masked:
            free = plan[3 + own_span] == 0
            q_t = lax.broadcasted_iota(jnp.int32, (group, keys_n), 0) % tok
            k_t = lax.broadcasted_iota(jnp.int32, (group, keys_n), 1)
            core = plan[2]
            k_pos = plan[1] * keys_n + jnp.where(
                k_t < tok, core * tok + k_t, (1 - core) * tok + k_t - tok
            )
        for c in chunks:
            s = dot_rows(q_rows[c, :], keys)
            if masked:
                q_xh = plan[1] if c.start < half else 1 - plan[1]
                q_pos = (q_xh * 2 + core) * tok + q_t
                s = jnp.where((k_pos <= q_pos) | free, s, NEG)
            score[i, c, :] = s
            row_max[c, :] = functools.reduce(jnp.maximum, lane_tiles(s), row_max[c, :])

    @pl.loop(0, count - 1)
    def _(i):
        score_block(i, False)

    score_block(count - 1, True)
    for c in chunks:
        top = jnp.max(row_max[c, :], axis=1, keepdims=True)
        row_max[c, :] = jnp.broadcast_to(top, (group, LANES))

    @pl.loop(0, count)
    def _(i):
        slot = order[i]
        values = jnp.concatenate([kv_mine[slot, :, dim:], kv_mate[slot, :, dim:]], axis=0)
        for c in chunks:
            top = row_max[c, :]
            tiles = [jnp.exp2(t - top) for t in lane_tiles(score[i, c, :])]
            row_sum[c, :] += functools.reduce(jnp.add, tiles)
            p = jnp.concatenate(tiles, axis=1).astype(jnp.bfloat16)
            prob[i, c, :] = p
            acc[c, :] += dot(p, values)

    lane = lax.broadcasted_iota(jnp.int32, (tok, LANES), 1)
    table = jnp.zeros((tok, LANES), jnp.float32)
    for j in range(2 * heads):
        r = slice(j * tok, (j + 1) * tok)
        grad = g_raw[r, :].astype(jnp.float32)
        table = jnp.where(lane == STATS * j, row_max[r, :], table)
        table = jnp.where(lane == STATS * j + 1, lane_sum(row_sum[r, :]), table)
        table = jnp.where(lane == STATS * j + 2, lane_sum(grad * acc[r, :]), table)
    stats[...] = jnp.transpose(table)[: stats.shape[0], :]


def backward(
    plan, prob, stats_own, stats_mate, acc_in, q_rows, g_raw, kv_mine, kv_mate,
    mix_keep, mix_give, dkv_keep, dkv_give,
    order, g_rows, ds_rows, delta_rows, acc,
    *, tok, heads, dim, group,
):
    spans = order.shape[0]
    count, _ = visible_slots(plan, order, spans)
    half = heads * tok
    inv_sqrt = 1.0 / math.sqrt(dim)
    mine, theirs = columns_of(stats_own[...]), columns_of(stats_mate[...])
    for j in range(2 * heads):
        r = slice(j * tok, (j + 1) * tok)
        h = slice((j % heads) * dim, (j % heads + 1) * dim)
        a, b = STATS * j, STATS * ((j + heads) % (2 * heads))
        top = jnp.maximum(mine[:, a : a + 1], theirs[:, b : b + 1])
        f_mine = jnp.exp2(mine[:, a : a + 1] - top)
        f_theirs = jnp.exp2(theirs[:, b : b + 1] - top)
        total = mine[:, a + 1 : a + 2] * f_mine + theirs[:, b + 1 : b + 2] * f_theirs
        scale = f_mine / total
        delta = (mine[:, a + 2 : a + 3] * f_mine + theirs[:, b + 2 : b + 3] * f_theirs) / total
        delta_rows[r, :] = jnp.broadcast_to(delta * scale, (tok, LANES))
        mix = mix_keep if j < heads else mix_give
        g_rows[r, :] = (g_raw[r, :].astype(jnp.float32) * scale).astype(jnp.bfloat16)
        mix[0, :, h] = (acc_in[r, :] * scale).astype(jnp.bfloat16)
    acc[...] = jnp.zeros_like(acc)
    chunks = [slice(r, r + group) for r in range(0, 2 * half, group)]

    _, lower, own_span = unpack(plan, spans)

    @pl.loop(0, spans)
    def _(slot):
        span = plan[3 + 2 * spans + slot]

        @pl.when((span < lower) | (span > own_span))
        def _():
            dkv_keep[slot] = jnp.zeros(dkv_keep.shape[1:], dkv_keep.dtype)
            dkv_give[slot] = jnp.zeros(dkv_give.shape[1:], dkv_give.dtype)

    @pl.loop(0, count)
    def _(i):
        slot = order[i]
        keys = jnp.concatenate([kv_mine[slot, :, :dim], kv_mate[slot, :, :dim]], axis=0)
        values = jnp.concatenate([kv_mine[slot, :, dim:], kv_mate[slot, :, dim:]], axis=0)
        for c in chunks:
            d_prob = dot_rows(g_rows[c, :], values)
            p = prob[i, c, :].astype(jnp.float32)
            delta = delta_rows[c, :]
            tiles = [x * (y - delta) for x, y in zip(lane_tiles(p), lane_tiles(d_prob))]
            ds = jnp.concatenate(tiles, axis=1).astype(jnp.bfloat16)
            ds_rows[c, :] = ds
            acc[c, :] += dot(ds, keys)
        d_keys = (dot_cols(ds_rows[...], q_rows[...]) * LN2).astype(jnp.bfloat16)
        d_values = dot_cols(prob[i], g_rows[...]).astype(jnp.bfloat16)
        dkv_keep[slot, :, :dim] = d_keys[:tok]
        dkv_keep[slot, :, dim:] = d_values[:tok]
        dkv_give[slot, :, :dim] = d_keys[tok:]
        dkv_give[slot, :, dim:] = d_values[tok:]

    for j in range(2 * heads):
        h = slice((j % heads) * dim, (j % heads + 1) * dim)
        mix = mix_keep if j < heads else mix_give
        mix[1, :, h] = (acc[j * tok : (j + 1) * tok, :] * inv_sqrt).astype(jnp.bfloat16)


def spread(keys, values, out):
    both = jnp.concatenate([keys[...], values[...]], axis=1)
    for n in range(out.shape[0]):
        out[n] = both


SMEM_SPEC = pl.BlockSpec(memory_space=pltpu.SMEM)
VMEM_SPEC = pl.BlockSpec(memory_space=pltpu.VMEM)


def sizes_of(q_raw, kv_mine):
    n_rows, dim = q_raw.shape
    spans, tok, _ = kv_mine.shape
    return spans, tok, dim, n_rows // (2 * tok), n_rows


def small_params(limit=SMALL_LIMIT):
    return pltpu.CompilerParams(vmem_limit_bytes=limit)


def row_squares_call(queries, q_mate):
    return pl.pallas_call(
        row_squares,
        out_shape=jax.ShapeDtypeStruct((2, queries.shape[0]), jnp.float32),
        in_specs=[VMEM_SPEC] * 2,
        out_specs=VMEM_SPEC,
        compiler_params=small_params(),
        cost_estimate=LONG,
        name="row_squares",
    )(queries, q_mate)


def prepare_call(queries, q_mate, out_grad, g_mate, dim):
    tok, local = queries.shape
    heads = local // dim
    rows = jax.ShapeDtypeStruct((2 * heads * tok, dim), jnp.bfloat16)
    return pl.pallas_call(
        functools.partial(prepare, tok=tok, heads=heads, dim=dim),
        out_shape=(rows, rows),
        in_specs=[VMEM_SPEC] * 4,
        out_specs=(VMEM_SPEC,) * 2,
        compiler_params=small_params(),
        cost_estimate=SHORT,
        name="prepare",
    )(queries, q_mate, out_grad, g_mate)


def merge_call(keep, got):
    part = jax.ShapeDtypeStruct(keep.shape[1:], jnp.bfloat16)
    return pl.pallas_call(
        merge,
        out_shape=(part, part),
        in_specs=[VMEM_SPEC] * 2,
        out_specs=(VMEM_SPEC,) * 2,
        compiler_params=small_params(),
        cost_estimate=LONG,
        name="merge",
    )(keep, got)


def forward_call(plan, square_sum, gain, q_raw, g_raw, kv_mine, kv_mate, width, group=384):
    spans, tok, dim, heads, n_rows = sizes_of(q_raw, kv_mine)
    stat_rows = -(-2 * heads * STATS // 16) * 16
    return pl.pallas_call(
        functools.partial(forward, tok=tok, heads=heads, dim=dim, group=group, width=width),
        out_shape=(
            jax.ShapeDtypeStruct((spans, n_rows, 2 * tok), jnp.bfloat16),
            jax.ShapeDtypeStruct((n_rows, dim), jnp.float32),
            jax.ShapeDtypeStruct((stat_rows, LANES), jnp.float32),
            jax.ShapeDtypeStruct((n_rows, dim), jnp.bfloat16),
        ),
        in_specs=[SMEM_SPEC] + [VMEM_SPEC] * 6,
        out_specs=(VMEM_SPEC,) * 4,
        scratch_shapes=[
            pltpu.SMEM((spans,), jnp.int32),
            pltpu.VMEM((spans, n_rows, 2 * tok), jnp.float32),
            pltpu.VMEM((n_rows, LANES), jnp.float32),
            pltpu.VMEM((n_rows, LANES), jnp.float32),
        ],
        compiler_params=pltpu.CompilerParams(vmem_limit_bytes=VMEM_LIMIT),
        name="attend_forward",
    )(plan, square_sum, gain, q_raw, g_raw, kv_mine, kv_mate)


def backward_call(
    plan, prob, stats_own, stats_mate, acc, q_rows, g_raw, kv_mine, kv_mate, group=384
):
    spans, tok, dim, heads, n_rows = sizes_of(q_rows, kv_mine)
    mix = jax.ShapeDtypeStruct((2, tok, heads * dim), jnp.bfloat16)
    part = jax.ShapeDtypeStruct(kv_mine.shape, jnp.bfloat16)
    return pl.pallas_call(
        functools.partial(backward, tok=tok, heads=heads, dim=dim, group=group),
        out_shape=(mix, mix, part, part),
        in_specs=[SMEM_SPEC] + [VMEM_SPEC] * 8,
        out_specs=(VMEM_SPEC,) * 4,
        scratch_shapes=[
            pltpu.SMEM((spans,), jnp.int32),
            pltpu.VMEM((n_rows, dim), jnp.bfloat16),
            pltpu.VMEM((n_rows, 2 * tok), jnp.bfloat16),
            pltpu.VMEM((n_rows, LANES), jnp.float32),
            pltpu.VMEM((n_rows, dim), jnp.float32),
        ],
        compiler_params=pltpu.CompilerParams(vmem_limit_bytes=VMEM_LIMIT),
        name="attend_backward",
    )(plan, prob, stats_own, stats_mate, acc, q_rows, g_raw, kv_mine, kv_mate)


def spread_call(keys, values, n_z):
    tok, dim = keys.shape
    return pl.pallas_call(
        spread,
        out_shape=jax.ShapeDtypeStruct((n_z, tok, 2 * dim), jnp.bfloat16),
        in_specs=[VMEM_SPEC] * 2,
        out_specs=VMEM_SPEC,
        name="spread",
    )(keys, values)


def head_sum(x):
    x = x + lax.ppermute(x, "xl", SWAP)
    n = lax.axis_size("y")
    others = [lax.ppermute(x, "y", [(i, (i + d) % n) for i in range(n)]) for d in range(1, n)]
    return functools.reduce(jnp.add, others, x)


def shards(
    queries, key_states, value_states, out_grad, norm_gain, mask_kind, range_start, placement
):
    tok, local = queries.shape
    dim = key_states.shape[1]
    n_heads = lax.axis_size(HEAD)
    n_z = lax.axis_size("z")
    places = [lax.axis_index(a).astype(jnp.int32)[None] for a in CTX]
    plan = jnp.concatenate(places + [mask_kind, range_start, placement])

    q_mate = lax.ppermute(queries, "xh", SWAP)
    g_mate = lax.ppermute(out_grad, "xh", SWAP)
    kv_mine = lax.all_to_all(spread_call(key_states, value_states, n_z), "z", 0, 0)
    square_sum = head_sum(row_squares_call(queries, q_mate))
    q_raw, g_raw = prepare_call(queries, q_mate, out_grad, g_mate, dim)
    kv_mine, square_sum, q_raw, g_raw = lax.optimization_barrier(
        (kv_mine, square_sum, q_raw, g_raw)
    )
    kv_mate = lax.ppermute(kv_mine, "core", SWAP)

    prob, acc, stats, q_rows = forward_call(
        plan, square_sum, norm_gain[None, :], q_raw, g_raw, kv_mine, kv_mate, local * n_heads
    )
    stats_mate = lax.ppermute(stats, "xh", SWAP)
    mix_keep, mix_give, dkv_keep, dkv_give = backward_call(
        plan, prob, stats, stats_mate, acc, q_rows, g_raw, kv_mine, kv_mate
    )
    mix_got = lax.ppermute(mix_give, "xh", SWAP)
    dkv_got = lax.ppermute(dkv_give, "core", SWAP)
    chip = (dkv_keep.astype(jnp.float32) + dkv_got.astype(jnp.float32)).astype(jnp.bfloat16)
    pieces = lax.all_to_all(chip, "z", 0, 0)
    total = jnp.sum(pieces.astype(jnp.float32), axis=0).astype(jnp.bfloat16)
    attn_out, d_queries = merge_call(mix_keep, mix_got)
    return (attn_out, d_queries, total[:, :dim], total[:, dim:])


def solution(mesh):
    fine = Mesh(mesh.devices.reshape(8, 2, 2, 4, 2), ("z", "xh", "core", "y", "xl"))
    rows = P(CTX, HEAD)
    in_specs = (rows, rows, rows, rows, P(HEAD), P(), P(), P())
    out_specs = (rows, rows, rows, rows)
    return jax.shard_map(shards, mesh=fine, in_specs=in_specs, out_specs=out_specs, check_vma=False)
```

```python
import functools
import math

import jax
import jax.numpy as jnp
from jax import lax
from jax.experimental import pallas as pl
from jax.experimental.pallas import tpu as pltpu
from jax.sharding import Mesh
from jax.sharding import PartitionSpec as P

NEG = -1e30
EPS = 1e-06
LOG2E = 1.4426950408889634
LN2 = 0.6931471805599453
LANES = 128
STATS = 3

CTX = ("z", "xh", "core")
HEAD = ("y", "xl")
SWAP = [(0, 1), (1, 0)]
VMEM_LIMIT = 48 * 2**20
SMALL_LIMIT = 8 * 2**20
LONG = pl.CostEstimate(flops=2 * 10**10, bytes_accessed=2**20, transcendentals=0)
SHORT = pl.CostEstimate(flops=2**10, bytes_accessed=2**10, transcendentals=0)


def dot_rows(left_side, right_side):
    return lax.dot_general(
        left_side, right_side, (((1,), (1,)), ((), ())), preferred_element_type=jnp.float32
    )


def dot_cols(left_side, right_side):
    return lax.dot_general(
        left_side, right_side, (((0,), (0,)), ((), ())), preferred_element_type=jnp.float32
    )


def dot(left_side, right_side):
    return jnp.dot(left_side, right_side, preferred_element_type=jnp.float32)


def lane_tiles(x):
    return [x[:, j : j + LANES] for j in range(0, x.shape[1], LANES)]


def lane_sum(x):
    return jnp.sum(x, axis=1, keepdims=True)


def unpack(plan, spans):
    own_span = plan[3 + 2 * spans + plan[0]]
    lower = plan[3 + spans + own_span]
    return own_span - lower + 1, lower, own_span


def visible_slots(plan, order, spans):
    count, lower, own_span = unpack(plan, spans)

    @pl.loop(0, spans)
    def _(slot):
        span = plan[3 + 2 * spans + slot]

        @pl.when((lower <= span) & (span < own_span))
        def _():
            order[span - lower + 1] = slot

    order[0] = plan[0]

    return count, own_span


def stacked(order, first, n, lanes, kv_mine, kv_mate):
    parts = []
    for k in range(n):
        slot = order[first + k]
        parts += [kv_mine[slot, :, lanes], kv_mate[slot, :, lanes]]
    return jnp.concatenate(parts, axis=0)


def by_pairs(count, body):
    @pl.loop(0, count // 2)
    def _(i):
        body(2 * i, 2)

    @pl.when(count % 2 == 1)
    def _():
        body(count - 1, 1)


def columns_of(table):
    pad = jnp.zeros((LANES - table.shape[0], LANES), jnp.float32)
    return jnp.transpose(jnp.concatenate([table, pad], axis=0))


def row_squares(queries, q_mate, parts):
    for side, rows_of in enumerate((queries, q_mate)):
        wide = rows_of[...].astype(jnp.float32)
        total = functools.reduce(jnp.add, lane_tiles(wide * wide))
        parts[side : side + 1, :] = jnp.sum(jnp.transpose(total), axis=0, keepdims=True)


def prepare(queries, q_mate, out_grad, g_mate, q_raw, g_raw, *, tok, heads, dim):
    for side, (q_part, g_part) in enumerate(((queries, out_grad), (q_mate, g_mate))):
        for h in range(heads):
            first = (side * heads + h) * tok
            q_raw[first : first + tok, :] = q_part[:, h * dim : (h + 1) * dim]
            g_raw[first : first + tok, :] = g_part[:, h * dim : (h + 1) * dim]


def merge(out_keep, out_got, dq_keep, dq_got, out, dq):
    out[...] = (out_keep[...].astype(jnp.float32) + out_got[...].astype(jnp.float32)).astype(out.dtype)
    dq[...] = (dq_keep[...].astype(jnp.float32) + dq_got[...].astype(jnp.float32)).astype(dq.dtype)


def forward(
    plan, square_sum, gain, q_raw, g_raw, kv_mine, kv_mate,
    prob_out, acc, stats, q_rows,
    order, score, prob, row_max, row_sum, sems,
    *, tok, heads, dim, group, width,
):
    spans = order.shape[0]
    half = heads * tok
    keys_n = 2 * tok
    sums = columns_of(square_sum[...])
    scale = lax.rsqrt(sums / width + EPS) * (LOG2E / math.sqrt(dim))
    for side in range(2):
        for h in range(heads):
            r = slice(side * half + h * tok, side * half + (h + 1) * tok)
            normed = q_raw[r, :].astype(jnp.float32) * scale[:, side : side + 1]
            normed = normed * gain[:, h * dim : (h + 1) * dim]
            q_rows[r, :] = normed.astype(jnp.bfloat16)
    count, own_span = visible_slots(plan, order, spans)
    row_max[...] = jnp.full_like(row_max, NEG)
    row_sum[...] = jnp.zeros_like(row_sum)
    acc[...] = jnp.zeros_like(acc)
    chunks = [slice(r, r + group) for r in range(0, 2 * half, group)]

    def score_block(i, masked):
        slot = order[i]
        keys = jnp.concatenate([kv_mine[slot, :, :dim], kv_mate[slot, :, :dim]], axis=0)
        if masked:
            free = plan[3 + own_span] == 0
            q_t = lax.broadcasted_iota(jnp.int32, (group, keys_n), 0) % tok
            k_t = lax.broadcasted_iota(jnp.int32, (group, keys_n), 1)
            core = plan[2]
            k_pos = plan[1] * keys_n + jnp.where(
                k_t < tok, core * tok + k_t, (1 - core) * tok + k_t - tok
            )
        for c in chunks:
            s = dot_rows(q_rows[c, :], keys)
            if masked:
                q_xh = plan[1] if c.start < half else 1 - plan[1]
                q_pos = (q_xh * 2 + core) * tok + q_t
                s = jnp.where((k_pos <= q_pos) | free, s, NEG)
            score[i, c, :] = s
            row_max[c, :] = functools.reduce(jnp.maximum, lane_tiles(s), row_max[c, :])

    score_block(0, True)

    def score_blocks(first, n):
        keys = stacked(order, first, n, slice(0, dim), kv_mine, kv_mate)
        for c in chunks:
            s = dot_rows(q_rows[c, :], keys)
            for k in range(n):
                score[first + k, c, :] = s[:, k * keys_n : (k + 1) * keys_n]
            row_max[c, :] = functools.reduce(jnp.maximum, lane_tiles(s), row_max[c, :])

    by_pairs(count - 1, lambda first, n: score_blocks(first + 1, n))

    for c in chunks:
        top = jnp.max(row_max[c, :], axis=1, keepdims=True)
        row_max[c, :] = jnp.broadcast_to(top, (group, LANES))

    def weigh(first, n):
        values = stacked(order, first, n, slice(dim, 2 * dim), kv_mine, kv_mate)
        for c in chunks:
            top = row_max[c, :]
            blocks = [lane_tiles(score[first + k, c, :]) for k in range(n)]
            tiles = [[jnp.exp2(t - top) for t in b] for b in blocks]
            row_sum[c, :] += functools.reduce(jnp.add, sum(tiles, []))
            p = [jnp.concatenate(b, axis=1).astype(jnp.bfloat16) for b in tiles]
            for k in range(n):
                prob[first + k, c, :] = p[k]
            acc[c, :] += dot(jnp.concatenate(p, axis=1), values)
        for k in range(n):
            b = first + k
            pltpu.make_async_copy(prob.at[b], prob_out.at[b], sems.at[b]).start()

    by_pairs(count, weigh)

    lane = lax.broadcasted_iota(jnp.int32, (tok, LANES), 1)
    table = jnp.zeros((tok, LANES), jnp.float32)
    for j in range(2 * heads):
        r = slice(j * tok, (j + 1) * tok)
        grad = g_raw[r, :].astype(jnp.float32)
        table = jnp.where(lane == STATS * j, row_max[r, :], table)
        table = jnp.where(lane == STATS * j + 1, lane_sum(row_sum[r, :]), table)
        table = jnp.where(lane == STATS * j + 2, lane_sum(grad * acc[r, :]), table)
    stats[...] = jnp.transpose(table)[: stats.shape[0], :]

    @pl.loop(0, count)
    def _(b):
        pltpu.make_async_copy(prob.at[b], prob_out.at[b], sems.at[b]).wait()


def backward(
    plan, prob_in, stats_own, stats_mate, acc_in, q_rows, g_raw, kv_mine, kv_mate,
    out_keep, out_give, ds_out, dkv_keep, dkv_give,
    order, g_rows, prob, ds_rows, delta_rows, q_cols, g_cols, in_sems, sems,
    *, tok, heads, dim, group,
):
    spans = order.shape[0]
    count, _ = visible_slots(plan, order, spans)

    @pl.loop(0, count)
    def _(b):
        pltpu.make_async_copy(prob_in.at[b], prob.at[b], in_sems.at[b]).start()

    half = heads * tok
    mine, theirs = columns_of(stats_own[...]), columns_of(stats_mate[...])
    for j in range(2 * heads):
        r = slice(j * tok, (j + 1) * tok)
        h = slice((j % heads) * dim, (j % heads + 1) * dim)
        a, b = STATS * j, STATS * ((j + heads) % (2 * heads))
        top = jnp.maximum(mine[:, a : a + 1], theirs[:, b : b + 1])
        f_mine = jnp.exp2(mine[:, a : a + 1] - top)
        f_theirs = jnp.exp2(theirs[:, b : b + 1] - top)
        total = mine[:, a + 1 : a + 2] * f_mine + theirs[:, b + 1 : b + 2] * f_theirs
        scale = f_mine / total
        delta = (mine[:, a + 2 : a + 3] * f_mine + theirs[:, b + 2 : b + 3] * f_theirs) / total
        delta_rows[r, :] = jnp.broadcast_to(delta * scale, (tok, LANES))
        out = out_keep if j < heads else out_give
        g_rows[r, :] = (g_raw[r, :].astype(jnp.float32) * scale).astype(jnp.bfloat16)
        out[:, h] = (acc_in[r, :] * scale).astype(jnp.bfloat16)
    for j in range(2 * heads):
        r = slice(j * tok, (j + 1) * tok)
        q_cols[:, r] = jnp.transpose(q_rows[r, :])
        g_cols[:, r] = jnp.transpose(g_rows[r, :])
    chunks = [slice(r, r + group) for r in range(0, 2 * half, group)]

    _, lower, own_span = unpack(plan, spans)

    @pl.loop(0, spans)
    def _(slot):
        span = plan[3 + 2 * spans + slot]

        @pl.when((span < lower) | (span > own_span))
        def _():
            dkv_keep[slot] = jnp.zeros(dkv_keep.shape[1:], dkv_keep.dtype)
            dkv_give[slot] = jnp.zeros(dkv_give.shape[1:], dkv_give.dtype)

    def grads_of(first, n):
        values = stacked(order, first, n, slice(dim, 2 * dim), kv_mine, kv_mate)
        for k in range(n):
            b = first + k
            pltpu.make_async_copy(prob_in.at[b], prob.at[b], in_sems.at[b]).wait()
        for c in chunks:
            d_prob = lane_tiles(dot_rows(g_rows[c, :], values))
            delta = delta_rows[c, :]
            p = sum([lane_tiles(prob[first + k, c, :].astype(jnp.float32)) for k in range(n)], [])
            tiles = [x * (y - delta) for x, y in zip(p, d_prob)]
            per = len(tiles) // n
            for k in range(n):
                block = jnp.concatenate(tiles[k * per : (k + 1) * per], axis=1)
                ds_rows[first + k, c, :] = block.astype(jnp.bfloat16)
        for k in range(n):
            b = first + k
            pltpu.make_async_copy(ds_rows.at[b], ds_out.at[b], sems.at[b]).start()
            slot = order[first + k]
            d_keys = jnp.transpose(dot(q_cols[...], ds_rows[first + k]) * LN2)
            d_keys = d_keys.astype(jnp.bfloat16)
            d_values = jnp.transpose(dot(g_cols[...], prob[first + k])).astype(jnp.bfloat16)
            dkv_keep[slot, :, :dim] = d_keys[:tok]
            dkv_keep[slot, :, dim:] = d_values[:tok]
            dkv_give[slot, :, :dim] = d_keys[tok:]
            dkv_give[slot, :, dim:] = d_values[tok:]

    by_pairs(count, grads_of)

    @pl.loop(0, count)
    def _(b):
        pltpu.make_async_copy(ds_rows.at[b], ds_out.at[b], sems.at[b]).wait()


def finish(
    plan, ds_in, kv_mine, kv_mate, dq_keep, dq_give, order, ds_rows, acc, sems,
    *, tok, heads, dim, group,
):
    count, _ = visible_slots(plan, order, order.shape[0])

    @pl.loop(0, count)
    def _(b):
        pltpu.make_async_copy(ds_in.at[b], ds_rows.at[b], sems.at[b]).start()

    half = heads * tok
    chunks = [slice(r, r + group) for r in range(0, 2 * half, group)]
    acc[...] = jnp.zeros_like(acc)

    def add(first, n):
        keys = stacked(order, first, n, slice(0, dim), kv_mine, kv_mate)
        for k in range(n):
            b = first + k
            pltpu.make_async_copy(ds_in.at[b], ds_rows.at[b], sems.at[b]).wait()
        for c in chunks:
            ds = jnp.concatenate([ds_rows[first + k, c, :] for k in range(n)], axis=1)
            acc[c, :] += dot(ds, keys)

    by_pairs(count, add)
    for j in range(2 * heads):
        h = slice((j % heads) * dim, (j % heads + 1) * dim)
        dq = dq_keep if j < heads else dq_give
        dq[:, h] = (acc[j * tok : (j + 1) * tok, :] / math.sqrt(dim)).astype(jnp.bfloat16)


def spread(keys, values, out):
    both = jnp.concatenate([keys[...], values[...]], axis=1)
    for n in range(out.shape[0]):
        out[n] = both


SMEM_SPEC = pl.BlockSpec(memory_space=pltpu.SMEM)
HBM_SPEC = pl.BlockSpec(memory_space=pltpu.HBM)
VMEM_SPEC = pl.BlockSpec(memory_space=pltpu.VMEM)


def sizes_of(q_raw, kv_mine):
    n_rows, dim = q_raw.shape
    spans, tok, _ = kv_mine.shape
    return spans, tok, dim, n_rows // (2 * tok), n_rows


def small_params(limit=SMALL_LIMIT):
    return pltpu.CompilerParams(vmem_limit_bytes=limit)


def row_squares_call(queries, q_mate):
    return pl.pallas_call(
        row_squares,
        out_shape=jax.ShapeDtypeStruct((2, queries.shape[0]), jnp.float32),
        in_specs=[VMEM_SPEC] * 2,
        out_specs=VMEM_SPEC,
        compiler_params=small_params(),
        cost_estimate=LONG,
        name="row_squares",
    )(queries, q_mate)


def prepare_call(queries, q_mate, out_grad, g_mate, dim):
    tok, local = queries.shape
    heads = local // dim
    rows = jax.ShapeDtypeStruct((2 * heads * tok, dim), jnp.bfloat16)
    return pl.pallas_call(
        functools.partial(prepare, tok=tok, heads=heads, dim=dim),
        out_shape=(rows, rows),
        in_specs=[VMEM_SPEC] * 4,
        out_specs=(VMEM_SPEC,) * 2,
        compiler_params=small_params(),
        cost_estimate=SHORT,
        name="prepare",
    )(queries, q_mate, out_grad, g_mate)


def merge_call(*parts):
    rows = jax.ShapeDtypeStruct(parts[0].shape, jnp.bfloat16)
    return pl.pallas_call(
        merge,
        out_shape=(rows, rows),
        in_specs=[VMEM_SPEC] * 4,
        out_specs=(VMEM_SPEC,) * 2,
        compiler_params=small_params(),
        cost_estimate=SHORT,
        name="merge",
    )(*parts)


def forward_call(plan, square_sum, gain, q_raw, g_raw, kv_mine, kv_mate, width, group=384):
    spans, tok, dim, heads, n_rows = sizes_of(q_raw, kv_mine)
    stat_rows = -(-2 * heads * STATS // 16) * 16
    return pl.pallas_call(
        functools.partial(forward, tok=tok, heads=heads, dim=dim, group=group, width=width),
        out_shape=(
            jax.ShapeDtypeStruct((spans, n_rows, 2 * tok), jnp.bfloat16),
            jax.ShapeDtypeStruct((n_rows, dim), jnp.float32),
            jax.ShapeDtypeStruct((stat_rows, LANES), jnp.float32),
            jax.ShapeDtypeStruct((n_rows, dim), jnp.bfloat16),
        ),
        in_specs=[SMEM_SPEC] + [VMEM_SPEC] * 6,
        out_specs=(HBM_SPEC, VMEM_SPEC, VMEM_SPEC, VMEM_SPEC),
        scratch_shapes=[
            pltpu.SMEM((spans,), jnp.int32),
            pltpu.VMEM((spans, n_rows, 2 * tok), jnp.float32),
            pltpu.VMEM((spans, n_rows, 2 * tok), jnp.bfloat16),
            pltpu.VMEM((n_rows, LANES), jnp.float32),
            pltpu.VMEM((n_rows, LANES), jnp.float32),
            pltpu.SemaphoreType.DMA((spans,)),
        ],
        compiler_params=pltpu.CompilerParams(vmem_limit_bytes=VMEM_LIMIT),
        name="attend_forward",
    )(plan, square_sum, gain, q_raw, g_raw, kv_mine, kv_mate)


def backward_call(
    plan, prob, stats_own, stats_mate, acc, q_rows, g_raw, kv_mine, kv_mate, group=768
):
    spans, tok, dim, heads, n_rows = sizes_of(q_rows, kv_mine)
    rows = jax.ShapeDtypeStruct((tok, heads * dim), jnp.bfloat16)
    part = jax.ShapeDtypeStruct(kv_mine.shape, jnp.bfloat16)
    return pl.pallas_call(
        functools.partial(backward, tok=tok, heads=heads, dim=dim, group=group),
        out_shape=(rows, rows, jax.ShapeDtypeStruct(prob.shape, jnp.bfloat16), part, part),
        in_specs=[SMEM_SPEC, HBM_SPEC] + [VMEM_SPEC] * 7,
        out_specs=(VMEM_SPEC, VMEM_SPEC, HBM_SPEC, VMEM_SPEC, VMEM_SPEC),
        scratch_shapes=[
            pltpu.SMEM((spans,), jnp.int32),
            pltpu.VMEM((n_rows, dim), jnp.bfloat16),
            pltpu.VMEM(prob.shape, jnp.bfloat16),
            pltpu.VMEM(prob.shape, jnp.bfloat16),
            pltpu.VMEM((n_rows, LANES), jnp.float32),
            pltpu.VMEM((dim, n_rows), jnp.bfloat16),
            pltpu.VMEM((dim, n_rows), jnp.bfloat16),
            pltpu.SemaphoreType.DMA((spans,)),
            pltpu.SemaphoreType.DMA((spans,)),
        ],
        compiler_params=small_params(VMEM_LIMIT),
        name="attend_backward",
    )(plan, prob, stats_own, stats_mate, acc, q_rows, g_raw, kv_mine, kv_mate)


def finish_call(plan, ds_rows, kv_mine, kv_mate, group=768):
    spans, n_rows, _ = ds_rows.shape
    _, tok, both = kv_mine.shape
    dim = both // 2
    heads = n_rows // (2 * tok)
    rows = jax.ShapeDtypeStruct((tok, heads * dim), jnp.bfloat16)
    return pl.pallas_call(
        functools.partial(finish, tok=tok, heads=heads, dim=dim, group=group),
        out_shape=(rows, rows),
        in_specs=[SMEM_SPEC, HBM_SPEC, VMEM_SPEC, VMEM_SPEC],
        out_specs=(VMEM_SPEC,) * 2,
        scratch_shapes=[
            pltpu.SMEM((spans,), jnp.int32),
            pltpu.VMEM(ds_rows.shape, jnp.bfloat16),
            pltpu.VMEM((n_rows, dim), jnp.float32),
            pltpu.SemaphoreType.DMA((spans,)),
        ],
        compiler_params=small_params(VMEM_LIMIT),
        cost_estimate=LONG,
        name="attend_finish",
    )(plan, ds_rows, kv_mine, kv_mate)


def spread_call(keys, values, n_z):
    tok, dim = keys.shape
    return pl.pallas_call(
        spread,
        out_shape=jax.ShapeDtypeStruct((n_z, tok, 2 * dim), jnp.bfloat16),
        in_specs=[VMEM_SPEC] * 2,
        out_specs=VMEM_SPEC,
        name="spread",
    )(keys, values)


def head_sum(x):
    x = x + lax.ppermute(x, "xl", SWAP)
    n = lax.axis_size("y")
    others = [lax.ppermute(x, "y", [(i, (i + d) % n) for i in range(n)]) for d in range(1, n)]
    return functools.reduce(jnp.add, others, x)


def shards(
    queries, key_states, value_states, out_grad, norm_gain, mask_kind, range_start, placement
):
    tok, local = queries.shape
    dim = key_states.shape[1]
    n_heads = lax.axis_size(HEAD)
    n_z = lax.axis_size("z")
    places = [lax.axis_index(a).astype(jnp.int32)[None] for a in CTX]
    plan = jnp.concatenate(places + [mask_kind, range_start, placement])

    q_mate = lax.ppermute(queries, "xh", SWAP)
    g_mate = lax.ppermute(out_grad, "xh", SWAP)
    kv_mine = lax.all_to_all(spread_call(key_states, value_states, n_z), "z", 0, 0)
    square_sum = head_sum(row_squares_call(queries, q_mate))
    q_raw, g_raw = prepare_call(queries, q_mate, out_grad, g_mate, dim)
    kv_mine, square_sum, q_raw, g_raw = lax.optimization_barrier(
        (kv_mine, square_sum, q_raw, g_raw)
    )
    kv_mate = lax.ppermute(kv_mine, "core", SWAP)

    prob, acc, stats, q_rows = forward_call(
        plan, square_sum, norm_gain[None, :], q_raw, g_raw, kv_mine, kv_mate, local * n_heads
    )
    stats_mate = lax.ppermute(stats, "xh", SWAP)
    out_keep, out_give, ds_rows, dkv_keep, dkv_give = backward_call(
        plan, prob, stats, stats_mate, acc, q_rows, g_raw, kv_mine, kv_mate
    )
    out_got = lax.ppermute(out_give, "xh", SWAP)
    dkv_got = lax.ppermute(dkv_give, "core", SWAP)
    chip = (dkv_keep.astype(jnp.float32) + dkv_got.astype(jnp.float32)).astype(jnp.bfloat16)
    chip, ds_rows = lax.optimization_barrier((chip, ds_rows))
    pieces = lax.all_to_all(chip, "z", 0, 0)
    dq_keep, dq_give = finish_call(plan, ds_rows, kv_mine, kv_mate)
    dq_got = lax.ppermute(dq_give, "xh", SWAP)
    attn_out, d_queries = merge_call(out_keep, out_got, dq_keep, dq_got)
    total = jnp.sum(pieces.astype(jnp.float32), axis=0).astype(jnp.bfloat16)
    return (attn_out, d_queries, total[:, :dim], total[:, dim:])


def solution(mesh):
    fine = Mesh(mesh.devices.reshape(8, 2, 2, 4, 2), ("z", "xh", "core", "y", "xl"))
    rows = P(CTX, HEAD)
    in_specs = (rows, rows, rows, rows, P(HEAD), P(), P(), P())
    out_specs = (rows, rows, rows, rows)
    return jax.shard_map(shards, mesh=fine, in_specs=in_specs, out_specs=out_specs, check_vma=False)
```

```python
import functools
import math

import jax
import jax.numpy as jnp
from jax import lax
from jax.experimental import pallas as pl
from jax.experimental.pallas import tpu as pltpu
from jax.sharding import Mesh
from jax.sharding import PartitionSpec as P

NEG = -1e30
EPS = 1e-06
LOG2E = 1.4426950408889634
LN2 = 0.6931471805599453
LANES = 128
STATS = 3

CTX = ("z", "xh", "core")
HEAD = ("y", "xl")
SWAP = [(0, 1), (1, 0)]
VMEM_LIMIT = 24 * 2**20
BACKWARD_LIMIT = 18 * 2**20
SMALL_LIMIT = 8 * 2**20
LONG = pl.CostEstimate(flops=2 * 10**10, bytes_accessed=2**20, transcendentals=0)
MEDIUM = pl.CostEstimate(flops=3 * 10**9, bytes_accessed=2**10, transcendentals=0)
SHORT = pl.CostEstimate(flops=2**10, bytes_accessed=2**10, transcendentals=0)


def dot_rows(left_side, right_side):
    return lax.dot_general(
        left_side, right_side, (((1,), (1,)), ((), ())), preferred_element_type=jnp.float32
    )


def dot_cols(left_side, right_side):
    return lax.dot_general(
        left_side, right_side, (((0,), (0,)), ((), ())), preferred_element_type=jnp.float32
    )


def dot(left_side, right_side):
    return jnp.dot(left_side, right_side, preferred_element_type=jnp.float32)


def lane_tiles(x):
    return [x[:, j : j + LANES] for j in range(0, x.shape[1], LANES)]


def lane_sum(x):
    return jnp.sum(x, axis=1, keepdims=True)


def unpack(plan, spans):
    own_span = plan[3 + 2 * spans + plan[0]]
    lower = plan[3 + spans + own_span]
    return own_span - lower + 1, lower, own_span


def visible_slots(plan, order, spans):
    count, lower, own_span = unpack(plan, spans)

    @pl.loop(0, spans)
    def _(slot):
        span = plan[3 + 2 * spans + slot]

        @pl.when((lower <= span) & (span < own_span))
        def _():
            order[span - lower + 1] = slot

    order[0] = plan[0]

    return count, own_span


def stacked(order, first, n, lanes, kv_mine, kv_mate):
    parts = []
    for k in range(n):
        slot = order[first + k]
        parts += [kv_mine[slot, :, lanes], kv_mate[slot, :, lanes]]
    return jnp.concatenate(parts, axis=0)


def by_pairs(count, body):
    @pl.loop(0, count // 2)
    def _(i):
        body(2 * i, 2)

    @pl.when(count % 2 == 1)
    def _():
        body(count - 1, 1)


def columns_of(table):
    pad = jnp.zeros((LANES - table.shape[0], LANES), jnp.float32)
    return jnp.transpose(jnp.concatenate([table, pad], axis=0))


def squares_of(rows_of):
    wide = rows_of.astype(jnp.float32)
    total = functools.reduce(jnp.add, lane_tiles(wide * wide))
    return jnp.sum(jnp.transpose(total), axis=0, keepdims=True)


def row_squares(own, q_mate, parts):
    parts[0:1, :] = own[...]
    parts[1:2, :] = squares_of(q_mate[...])


def normalize(square_sum, gain, q_raw, q_rows, q_cols, *, tok, heads, dim, width):
    sums = columns_of(square_sum[...])
    scale = lax.rsqrt(sums / width + EPS) * (LOG2E / math.sqrt(dim))
    for side in range(2):
        for h in range(heads):
            r = slice((side * heads + h) * tok, (side * heads + h + 1) * tok)
            normed = q_raw[r, :].astype(jnp.float32) * scale[:, side : side + 1]
            normed = (normed * gain[:, h * dim : (h + 1) * dim]).astype(jnp.bfloat16)
            q_rows[r, :] = normed
            q_cols[:, r] = jnp.transpose(normed)


def prepare(queries, q_mate, out_grad, g_mate, q_raw, g_raw, *, tok, heads, dim):
    for side, (q_part, g_part) in enumerate(((queries, out_grad), (q_mate, g_mate))):
        for h in range(heads):
            first = (side * heads + h) * tok
            q_raw[first : first + tok, :] = q_part[:, h * dim : (h + 1) * dim]
            g_raw[first : first + tok, :] = g_part[:, h * dim : (h + 1) * dim]


def merge(out_keep, out_got, dq_keep, dq_got, out, dq):
    out[...] = (out_keep[...].astype(jnp.float32) + out_got[...].astype(jnp.float32)).astype(out.dtype)
    dq[...] = (dq_keep[...].astype(jnp.float32) + dq_got[...].astype(jnp.float32)).astype(dq.dtype)


def forward(
    plan, q_rows, g_raw, kv_mine, kv_mate,
    prob, acc, stats,
    order, score, row_max, row_sum,
    *, tok, heads, dim, group,
):
    spans = order.shape[0]
    half = heads * tok
    keys_n = 2 * tok
    count, own_span = visible_slots(plan, order, spans)
    row_max[...] = jnp.full_like(row_max, NEG)
    row_sum[...] = jnp.zeros_like(row_sum)
    acc[...] = jnp.zeros_like(acc)
    chunks = [slice(r, r + group) for r in range(0, 2 * half, group)]

    def score_block(i, masked):
        slot = order[i]
        keys = jnp.concatenate([kv_mine[slot, :, :dim], kv_mate[slot, :, :dim]], axis=0)
        if masked:
            free = plan[3 + own_span] == 0
            q_t = lax.broadcasted_iota(jnp.int32, (group, keys_n), 0) % tok
            k_t = lax.broadcasted_iota(jnp.int32, (group, keys_n), 1)
            core = plan[2]
            k_pos = plan[1] * keys_n + jnp.where(
                k_t < tok, core * tok + k_t, (1 - core) * tok + k_t - tok
            )
        for c in chunks:
            s = dot_rows(q_rows[c, :], keys)
            if masked:
                q_xh = plan[1] if c.start < half else 1 - plan[1]
                q_pos = (q_xh * 2 + core) * tok + q_t
                s = jnp.where((k_pos <= q_pos) | free, s, NEG)
            score[i, c, :] = s
            row_max[c, :] = functools.reduce(jnp.maximum, lane_tiles(s), row_max[c, :])

    score_block(0, True)

    def score_blocks(first, n):
        keys = stacked(order, first, n, slice(0, dim), kv_mine, kv_mate)
        for c in chunks:
            s = dot_rows(q_rows[c, :], keys)
            for k in range(n):
                score[first + k, c, :] = s[:, k * keys_n : (k + 1) * keys_n]
            row_max[c, :] = functools.reduce(jnp.maximum, lane_tiles(s), row_max[c, :])

    by_pairs(count - 1, lambda first, n: score_blocks(first + 1, n))

    for c in chunks:
        top = jnp.max(row_max[c, :], axis=1, keepdims=True)
        row_max[c, :] = jnp.broadcast_to(top, (group, LANES))

    def weigh(first, n):
        values = stacked(order, first, n, slice(dim, 2 * dim), kv_mine, kv_mate)
        for c in chunks:
            top = row_max[c, :]
            blocks = [lane_tiles(score[first + k, c, :]) for k in range(n)]
            tiles = [[jnp.exp2(t - top) for t in b] for b in blocks]
            row_sum[c, :] += functools.reduce(jnp.add, sum(tiles, []))
            p = [jnp.concatenate(b, axis=1).astype(jnp.bfloat16) for b in tiles]
            for k in range(n):
                prob[first + k, c, :] = p[k]
            acc[c, :] += dot(jnp.concatenate(p, axis=1), values)

    by_pairs(count, weigh)

    lane = lax.broadcasted_iota(jnp.int32, (tok, LANES), 1)
    table = jnp.zeros((tok, LANES), jnp.float32)
    for j in range(2 * heads):
        r = slice(j * tok, (j + 1) * tok)
        grad = g_raw[r, :].astype(jnp.float32)
        table = jnp.where(lane == STATS * j, row_max[r, :], table)
        table = jnp.where(lane == STATS * j + 1, lane_sum(row_sum[r, :]), table)
        table = jnp.where(lane == STATS * j + 2, lane_sum(grad * acc[r, :]), table)
    stats[...] = jnp.transpose(table)[: stats.shape[0], :]


def backward(
    plan, prob, stats_own, stats_mate, acc_in, q_cols, g_raw, kv_mine, kv_mate,
    out_keep, out_give, ds_out, dkv_keep, dkv_give,
    order, g_rows, ds_rows, delta_rows, g_cols, sems,
    *, tok, heads, dim, group,
):
    spans = order.shape[0]
    count, _ = visible_slots(plan, order, spans)

    half = heads * tok
    mine, theirs = columns_of(stats_own[...]), columns_of(stats_mate[...])
    for j in range(2 * heads):
        r = slice(j * tok, (j + 1) * tok)
        h = slice((j % heads) * dim, (j % heads + 1) * dim)
        a, b = STATS * j, STATS * ((j + heads) % (2 * heads))
        top = jnp.maximum(mine[:, a : a + 1], theirs[:, b : b + 1])
        f_mine = jnp.exp2(mine[:, a : a + 1] - top)
        f_theirs = jnp.exp2(theirs[:, b : b + 1] - top)
        total = mine[:, a + 1 : a + 2] * f_mine + theirs[:, b + 1 : b + 2] * f_theirs
        scale = f_mine / total
        delta = (mine[:, a + 2 : a + 3] * f_mine + theirs[:, b + 2 : b + 3] * f_theirs) / total
        delta_rows[r, :] = jnp.broadcast_to(delta * scale, (tok, LANES))
        out = out_keep if j < heads else out_give
        g_rows[r, :] = (g_raw[r, :].astype(jnp.float32) * scale).astype(jnp.bfloat16)
        out[:, h] = (acc_in[r, :] * scale).astype(jnp.bfloat16)
    for j in range(2 * heads):
        r = slice(j * tok, (j + 1) * tok)
        g_cols[:, r] = jnp.transpose(g_rows[r, :])
    chunks = [slice(r, r + group) for r in range(0, 2 * half, group)]

    _, lower, own_span = unpack(plan, spans)

    @pl.loop(0, spans)
    def _(slot):
        span = plan[3 + 2 * spans + slot]

        @pl.when((span < lower) | (span > own_span))
        def _():
            dkv_keep[slot] = jnp.zeros(dkv_keep.shape[1:], dkv_keep.dtype)
            dkv_give[slot] = jnp.zeros(dkv_give.shape[1:], dkv_give.dtype)

    def grads_of(first, n):
        values = stacked(order, first, n, slice(dim, 2 * dim), kv_mine, kv_mate)
        for c in chunks:
            d_prob = lane_tiles(dot_rows(g_rows[c, :], values))
            delta = delta_rows[c, :]
            p = sum([lane_tiles(prob[first + k, c, :].astype(jnp.float32)) for k in range(n)], [])
            tiles = [x * (y - delta) for x, y in zip(p, d_prob)]
            per = len(tiles) // n
            for k in range(n):
                block = jnp.concatenate(tiles[k * per : (k + 1) * per], axis=1)
                ds_rows[first + k, c, :] = block.astype(jnp.bfloat16)
        for k in range(n):
            b = first + k
            pltpu.make_async_copy(ds_rows.at[b], ds_out.at[b], sems.at[b]).start()

    def keys_of(first, n):
        for k in range(n):
            slot = order[first + k]
            d_keys = jnp.transpose(dot(q_cols[...], ds_rows[first + k]) * LN2)
            d_keys = d_keys.astype(jnp.bfloat16)
            dkv_keep[slot, :, :dim] = d_keys[:tok]
            dkv_give[slot, :, :dim] = d_keys[tok:]
            d_values = jnp.transpose(dot(g_cols[...], prob[first + k])).astype(jnp.bfloat16)
            dkv_keep[slot, :, dim:] = d_values[:tok]
            dkv_give[slot, :, dim:] = d_values[tok:]

    by_pairs(count, grads_of)
    by_pairs(count, keys_of)

    @pl.loop(0, count)
    def _(b):
        pltpu.make_async_copy(ds_rows.at[b], ds_out.at[b], sems.at[b]).wait()


def finish(
    plan, ds_in, kv_mine, kv_mate, dq_keep, dq_give, order, ds_rows, acc, sems,
    *, tok, heads, dim, group,
):
    count, _ = visible_slots(plan, order, order.shape[0])

    @pl.loop(0, count)
    def _(b):
        pltpu.make_async_copy(ds_in.at[b], ds_rows.at[b], sems.at[b]).start()


    half = heads * tok
    chunks = [slice(r, r + group) for r in range(0, 2 * half, group)]
    acc[...] = jnp.zeros_like(acc)

    def add(first, n):
        keys = stacked(order, first, n, slice(0, dim), kv_mine, kv_mate)
        for k in range(n):
            b = first + k
            pltpu.make_async_copy(ds_in.at[b], ds_rows.at[b], sems.at[b]).wait()
        for c in chunks:
            ds = jnp.concatenate([ds_rows[first + k, c, :] for k in range(n)], axis=1)
            acc[c, :] += dot(ds, keys)

    by_pairs(count, add)
    for j in range(2 * heads):
        h = slice((j % heads) * dim, (j % heads + 1) * dim)
        dq = dq_keep if j < heads else dq_give
        dq[:, h] = (acc[j * tok : (j + 1) * tok, :] / math.sqrt(dim)).astype(jnp.bfloat16)


def spread(keys, values, queries, out, squares):
    both = jnp.concatenate([keys[...], values[...]], axis=1)
    for n in range(out.shape[0]):
        out[n] = both
    squares[...] = squares_of(queries[...])


SMEM_SPEC = pl.BlockSpec(memory_space=pltpu.SMEM)
HBM_SPEC = pl.BlockSpec(memory_space=pltpu.HBM)
VMEM_SPEC = pl.BlockSpec(memory_space=pltpu.VMEM)


def sizes_of(q_raw, kv_mine):
    n_rows, dim = q_raw.shape
    spans, tok, _ = kv_mine.shape
    return spans, tok, dim, n_rows // (2 * tok), n_rows


def small_params(limit=SMALL_LIMIT):
    return pltpu.CompilerParams(vmem_limit_bytes=limit)


def row_squares_call(own, q_mate):
    return pl.pallas_call(
        row_squares,
        out_shape=jax.ShapeDtypeStruct((2, own.shape[1]), jnp.float32),
        in_specs=[VMEM_SPEC] * 2,
        out_specs=VMEM_SPEC,
        compiler_params=small_params(),
        cost_estimate=LONG,
        name="row_squares",
    )(own, q_mate)


def normalize_call(square_sum, gain, q_raw, width):
    tok = square_sum.shape[1]
    n_rows, dim = q_raw.shape
    return pl.pallas_call(
        functools.partial(
            normalize, tok=tok, heads=n_rows // (2 * tok), dim=dim, width=width
        ),
        out_shape=(
            jax.ShapeDtypeStruct((n_rows, dim), jnp.bfloat16),
            jax.ShapeDtypeStruct((dim, n_rows), jnp.bfloat16),
        ),
        in_specs=[VMEM_SPEC] * 3,
        out_specs=(VMEM_SPEC,) * 2,
        compiler_params=small_params(),
        cost_estimate=SHORT,
        name="normalize",
    )(square_sum, gain, q_raw)


def prepare_call(queries, q_mate, out_grad, g_mate, dim):
    tok, local = queries.shape
    heads = local // dim
    rows = jax.ShapeDtypeStruct((2 * heads * tok, dim), jnp.bfloat16)
    return pl.pallas_call(
        functools.partial(prepare, tok=tok, heads=heads, dim=dim),
        out_shape=(rows, rows),
        in_specs=[VMEM_SPEC] * 4,
        out_specs=(VMEM_SPEC,) * 2,
        compiler_params=small_params(),
        cost_estimate=SHORT,
        name="prepare",
    )(queries, q_mate, out_grad, g_mate)


def add_pair(one, other, out):
    out[...] = (one[...].astype(jnp.float32) + other[...].astype(jnp.float32)).astype(out.dtype)


def add_pair_call(one, other):
    return pl.pallas_call(
        add_pair,
        out_shape=jax.ShapeDtypeStruct(one.shape, jnp.bfloat16),
        in_specs=[VMEM_SPEC] * 2,
        out_specs=VMEM_SPEC,
        compiler_params=small_params(),
        name="add_pair",
    )(one, other)


def merge_call(*parts):
    rows = jax.ShapeDtypeStruct(parts[0].shape, jnp.bfloat16)
    return pl.pallas_call(
        merge,
        out_shape=(rows, rows),
        in_specs=[VMEM_SPEC] * 4,
        out_specs=(VMEM_SPEC,) * 2,
        compiler_params=small_params(),
        cost_estimate=SHORT,
        name="merge",
    )(*parts)


def forward_call(plan, q_rows, g_raw, kv_mine, kv_mate, group=384):
    spans, tok, dim, heads, n_rows = sizes_of(q_rows, kv_mine)
    stat_rows = -(-2 * heads * STATS // 16) * 16
    return pl.pallas_call(
        functools.partial(forward, tok=tok, heads=heads, dim=dim, group=group),
        out_shape=(
            jax.ShapeDtypeStruct((spans, n_rows, 2 * tok), jnp.bfloat16),
            jax.ShapeDtypeStruct((n_rows, dim), jnp.float32),
            jax.ShapeDtypeStruct((stat_rows, LANES), jnp.float32),
        ),
        in_specs=[SMEM_SPEC] + [VMEM_SPEC] * 4,
        out_specs=(VMEM_SPEC,) * 3,
        scratch_shapes=[
            pltpu.SMEM((spans,), jnp.int32),
            pltpu.VMEM((spans, n_rows, 2 * tok), jnp.float32),
            pltpu.VMEM((n_rows, LANES), jnp.float32),
            pltpu.VMEM((n_rows, LANES), jnp.float32),
        ],
        compiler_params=pltpu.CompilerParams(vmem_limit_bytes=VMEM_LIMIT),
        name="attend_forward",
    )(plan, q_rows, g_raw, kv_mine, kv_mate)


def backward_call(
    plan, prob, stats_own, stats_mate, acc, q_cols, g_raw, kv_mine, kv_mate, group=768
):
    spans, tok, dim, heads, n_rows = sizes_of(g_raw, kv_mine)
    rows = jax.ShapeDtypeStruct((tok, heads * dim), jnp.bfloat16)
    part = jax.ShapeDtypeStruct(kv_mine.shape, jnp.bfloat16)
    return pl.pallas_call(
        functools.partial(backward, tok=tok, heads=heads, dim=dim, group=group),
        out_shape=(rows, rows, pltpu.HBM(prob.shape, jnp.bfloat16), part, part),
        in_specs=[SMEM_SPEC] + [VMEM_SPEC] * 8,
        out_specs=(VMEM_SPEC, VMEM_SPEC, HBM_SPEC, VMEM_SPEC, VMEM_SPEC),
        scratch_shapes=[
            pltpu.SMEM((spans,), jnp.int32),
            pltpu.VMEM((n_rows, dim), jnp.bfloat16),
            pltpu.VMEM(prob.shape, jnp.bfloat16),
            pltpu.VMEM((n_rows, LANES), jnp.float32),
            pltpu.VMEM((dim, n_rows), jnp.bfloat16),
            pltpu.SemaphoreType.DMA((spans,)),
        ],
        compiler_params=small_params(BACKWARD_LIMIT),
        name="attend_backward",
    )(plan, prob, stats_own, stats_mate, acc, q_cols, g_raw, kv_mine, kv_mate)


def finish_call(plan, ds_rows, kv_mine, kv_mate, group=768):
    spans, n_rows, _ = ds_rows.shape
    _, tok, both = kv_mine.shape
    dim = both // 2
    heads = n_rows // (2 * tok)
    rows = jax.ShapeDtypeStruct((tok, heads * dim), jnp.bfloat16)
    return pl.pallas_call(
        functools.partial(finish, tok=tok, heads=heads, dim=dim, group=group),
        out_shape=(rows, rows),
        in_specs=[SMEM_SPEC, HBM_SPEC, VMEM_SPEC, VMEM_SPEC],
        out_specs=(VMEM_SPEC,) * 2,
        scratch_shapes=[
            pltpu.SMEM((spans,), jnp.int32),
            pltpu.VMEM(ds_rows.shape, jnp.bfloat16),
            pltpu.VMEM((n_rows, dim), jnp.float32),
            pltpu.SemaphoreType.DMA((spans,)),
        ],
        compiler_params=small_params(BACKWARD_LIMIT),
        cost_estimate=MEDIUM,
        name="attend_finish",
    )(plan, ds_rows, kv_mine, kv_mate)


def spread_call(keys, values, queries, n_z):
    tok, dim = keys.shape
    return pl.pallas_call(
        spread,
        out_shape=(
            jax.ShapeDtypeStruct((n_z, tok, 2 * dim), jnp.bfloat16),
            jax.ShapeDtypeStruct((1, tok), jnp.float32),
        ),
        in_specs=[VMEM_SPEC] * 3,
        out_specs=(VMEM_SPEC,) * 2,
        name="spread",
    )(keys, values, queries)


def head_sum(x):
    x = x + lax.ppermute(x, "xl", SWAP)
    n = lax.axis_size("y")
    others = [lax.ppermute(x, "y", [(i, (i + d) % n) for i in range(n)]) for d in range(1, n)]
    return functools.reduce(jnp.add, others, x)


def shards(
    queries, key_states, value_states, out_grad, norm_gain, mask_kind, range_start, placement
):
    tok, local = queries.shape
    dim = key_states.shape[1]
    n_heads = lax.axis_size(HEAD)
    n_z = lax.axis_size("z")
    places = [lax.axis_index(a).astype(jnp.int32)[None] for a in CTX]
    plan = jnp.concatenate(places + [mask_kind, range_start, placement])

    q_mate = lax.ppermute(queries, "xh", SWAP)
    g_mate = lax.ppermute(out_grad, "xh", SWAP)
    kv_out, own_squares = spread_call(key_states, value_states, queries, n_z)
    kv_mine = lax.all_to_all(kv_out, "z", 0, 0)
    square_sum = head_sum(row_squares_call(own_squares, q_mate))
    q_raw, g_raw = prepare_call(queries, q_mate, out_grad, g_mate, dim)
    kv_mine, square_sum, q_raw, g_raw = lax.optimization_barrier(
        (kv_mine, square_sum, q_raw, g_raw)
    )
    kv_mate = lax.ppermute(kv_mine, "core", SWAP)

    q_rows, q_cols = normalize_call(square_sum, norm_gain[None, :], q_raw, local * n_heads)
    prob, acc, stats = forward_call(plan, q_rows, g_raw, kv_mine, kv_mate)
    stats_mate = lax.ppermute(stats, "xh", SWAP)
    out_keep, out_give, ds_rows, dkv_keep, dkv_give = backward_call(
        plan, prob, stats, stats_mate, acc, q_cols, g_raw, kv_mine, kv_mate
    )
    out_got = lax.ppermute(out_give, "xh", SWAP)
    dkv_got = lax.ppermute(dkv_give, "core", SWAP)
    chip = add_pair_call(dkv_keep, dkv_got)
    chip, ds_rows = lax.optimization_barrier((chip, ds_rows))
    pieces = lax.all_to_all(chip, "z", 0, 0)
    ds_rows = pltpu.with_memory_space_constraint(ds_rows, pltpu.HBM)
    dq_keep, dq_give = finish_call(plan, ds_rows, kv_mine, kv_mate)
    dq_got = lax.ppermute(dq_give, "xh", SWAP)
    attn_out, d_queries = merge_call(out_keep, out_got, dq_keep, dq_got)
    total = jnp.sum(pieces.astype(jnp.float32), axis=0).astype(jnp.bfloat16)
    return (attn_out, d_queries, total[:, :dim], total[:, dim:])


def solution(mesh):
    fine = Mesh(mesh.devices.reshape(8, 2, 2, 4, 2), ("z", "xh", "core", "y", "xl"))
    rows = P(CTX, HEAD)
    in_specs = (rows, rows, rows, rows, P(HEAD), P(), P(), P())
    out_specs = (rows, rows, rows, rows)
    return jax.shard_map(shards, mesh=fine, in_specs=in_specs, out_specs=out_specs, check_vma=False)
```

```python
import functools
import math

import jax
import jax.numpy as jnp
from jax import lax
from jax.experimental import pallas as pl
from jax.experimental.pallas import tpu as pltpu
from jax.sharding import Mesh
from jax.sharding import PartitionSpec as P

NEG = -1e30
EPS = 1e-06
LOG2E = 1.4426950408889634
LN2 = 0.6931471805599453
LANES = 128
STATS = 3
STAT_ROWS = 16

CTX = ("z", "xh", "core")
HEAD = ("y", "xl")
SWAP = [(0, 1), (1, 0)]
VMEM_LIMIT = 24 * 2**20
BACKWARD_LIMIT = 18 * 2**20
SMALL_LIMIT = 9 * 2**20
LONG = pl.CostEstimate(flops=2 * 10**10, bytes_accessed=2**20, transcendentals=0)
MEDIUM = pl.CostEstimate(flops=3 * 10**9, bytes_accessed=2**10, transcendentals=0)
SHORT = pl.CostEstimate(flops=2**10, bytes_accessed=2**10, transcendentals=0)


def dot_rows(left_side, right_side):
    return lax.dot_general(
        left_side, right_side, (((1,), (1,)), ((), ())), preferred_element_type=jnp.float32
    )


def dot_cols(left_side, right_side):
    return lax.dot_general(
        left_side, right_side, (((0,), (0,)), ((), ())), preferred_element_type=jnp.float32
    )


def dot(left_side, right_side):
    return jnp.dot(left_side, right_side, preferred_element_type=jnp.float32)


def lane_tiles(x):
    return [x[:, j : j + LANES] for j in range(0, x.shape[1], LANES)]


def lane_sum(x):
    return jnp.sum(x, axis=1, keepdims=True)


def unpack(plan, spans):
    own_span = plan[3 + 2 * spans + plan[0]]
    lower = plan[3 + spans + own_span]
    return own_span - lower + 1, lower, own_span


def visible_slots(plan, order, spans):
    count, lower, own_span = unpack(plan, spans)

    @pl.loop(0, spans)
    def _(slot):
        span = plan[3 + 2 * spans + slot]

        @pl.when((lower <= span) & (span < own_span))
        def _():
            order[span - lower + 1] = slot

    order[0] = plan[0]

    return count, own_span


def stacked(order, first, n, lanes, kv_mine, kv_mate):
    parts = []
    for k in range(n):
        slot = order[first + k]
        parts += [kv_mine[slot, :, lanes], kv_mate[slot, :, lanes]]
    return jnp.concatenate(parts, axis=0)


def by_pairs(count, body):
    @pl.loop(0, count // 2)
    def _(i):
        body(2 * i, 2)

    @pl.when(count % 2 == 1)
    def _():
        body(count - 1, 1)


def columns_of(table):
    pad = jnp.zeros((LANES - table.shape[0], LANES), jnp.float32)
    return jnp.transpose(jnp.concatenate([table, pad], axis=0))


def squares_of(rows_of):
    wide = rows_of.astype(jnp.float32)
    total = functools.reduce(jnp.add, lane_tiles(wide * wide))
    return jnp.sum(jnp.transpose(total), axis=0, keepdims=True)


def row_squares(own, q_mate, parts):
    parts[0:1, :] = own[...]
    parts[1:2, :] = squares_of(q_mate[...])


def normalize(square_sum, gain, q_raw, q_rows, q_cols, *, tok, heads, dim, width):
    sums = columns_of(square_sum[...])
    scale = lax.rsqrt(sums / width + EPS) * (LOG2E / math.sqrt(dim))
    for side in range(2):
        for h in range(heads):
            r = slice((side * heads + h) * tok, (side * heads + h + 1) * tok)
            normed = q_raw[r, :].astype(jnp.float32) * scale[:, side : side + 1]
            normed = (normed * gain[:, h * dim : (h + 1) * dim]).astype(jnp.bfloat16)
            q_rows[r, :] = normed
            q_cols[:, r] = jnp.transpose(normed)


def prepare(queries, q_mate, out_grad, g_mate, q_raw, g_raw, *, tok, heads, dim):
    for side, (q_part, g_part) in enumerate(((queries, out_grad), (q_mate, g_mate))):
        for h in range(heads):
            first = (side * heads + h) * tok
            q_raw[first : first + tok, :] = q_part[:, h * dim : (h + 1) * dim]
            g_raw[first : first + tok, :] = g_part[:, h * dim : (h + 1) * dim]


def merge(out_keep, out_got, dq_keep, dq_got, out, dq):
    out[...] = (out_keep[...].astype(jnp.float32) + out_got[...].astype(jnp.float32)).astype(out.dtype)
    dq[...] = (dq_keep[...].astype(jnp.float32) + dq_got[...].astype(jnp.float32)).astype(dq.dtype)


def forward(
    plan, q_rows, g_raw, kv_mine, kv_mate,
    prob, acc, stats,
    order, score, row_max, row_sum,
    *, tok, heads, dim, group,
):
    spans = order.shape[0]
    half = heads * tok
    keys_n = 2 * tok
    count, own_span = visible_slots(plan, order, spans)
    row_max[...] = jnp.full_like(row_max, NEG)
    row_sum[...] = jnp.zeros_like(row_sum)
    acc[...] = jnp.zeros_like(acc)
    chunks = [slice(r, r + group) for r in range(0, 2 * half, group)]

    def score_block(i, masked):
        slot = order[i]
        keys = jnp.concatenate([kv_mine[slot, :, :dim], kv_mate[slot, :, :dim]], axis=0)
        if masked:
            free = plan[3 + own_span] == 0
            q_t = lax.broadcasted_iota(jnp.int32, (group, keys_n), 0) % tok
            k_t = lax.broadcasted_iota(jnp.int32, (group, keys_n), 1)
            core = plan[2]
            k_pos = plan[1] * keys_n + jnp.where(
                k_t < tok, core * tok + k_t, (1 - core) * tok + k_t - tok
            )
        for c in chunks:
            s = dot_rows(q_rows[c, :], keys)
            if masked:
                q_xh = plan[1] if c.start < half else 1 - plan[1]
                q_pos = (q_xh * 2 + core) * tok + q_t
                s = jnp.where((k_pos <= q_pos) | free, s, NEG)
            score[i, c, :] = s
            row_max[c, :] = functools.reduce(jnp.maximum, lane_tiles(s), row_max[c, :])

    score_block(0, True)

    def score_blocks(first, n):
        keys = stacked(order, first, n, slice(0, dim), kv_mine, kv_mate)
        for c in chunks:
            s = dot_rows(q_rows[c, :], keys)
            for k in range(n):
                score[first + k, c, :] = s[:, k * keys_n : (k + 1) * keys_n]
            row_max[c, :] = functools.reduce(jnp.maximum, lane_tiles(s), row_max[c, :])

    by_pairs(count - 1, lambda first, n: score_blocks(first + 1, n))

    for c in chunks:
        top = jnp.max(row_max[c, :], axis=1, keepdims=True)
        row_max[c, :] = jnp.broadcast_to(top, (group, LANES))

    def weigh(first, n):
        values = stacked(order, first, n, slice(dim, 2 * dim), kv_mine, kv_mate)
        for c in chunks:
            top = row_max[c, :]
            blocks = [lane_tiles(score[first + k, c, :]) for k in range(n)]
            tiles = [[jnp.exp2(t - top) for t in b] for b in blocks]
            row_sum[c, :] += functools.reduce(jnp.add, sum(tiles, []))
            p = [jnp.concatenate(b, axis=1).astype(jnp.bfloat16) for b in tiles]
            for k in range(n):
                prob[first + k, c, :] = p[k]
            acc[c, :] += dot(jnp.concatenate(p, axis=1), values)

    by_pairs(count, weigh)

    lane = lax.broadcasted_iota(jnp.int32, (tok, LANES), 1)
    table = jnp.zeros((tok, LANES), jnp.float32)
    for j in range(2 * heads):
        r = slice(j * tok, (j + 1) * tok)
        grad = g_raw[r, :].astype(jnp.float32)
        columns = (row_max[r, :], lane_sum(row_sum[r, :]), lane_sum(grad * acc[r, :]))
        for k, column in enumerate(columns):
            table = jnp.where(lane == STAT_ROWS * k + j, column, table)
    stats[...] = jnp.transpose(table)[: stats.shape[0], :]


def backward(
    plan, prob, stats_own, stats_mate, acc_in, q_cols, g_raw, kv_mine, kv_mate,
    out_keep, out_give, ds_out, dkv_keep, dkv_give,
    order, g_rows, ds_rows, delta_rows, g_cols, sems,
    *, tok, heads, dim, group,
):
    spans = order.shape[0]
    count, _ = visible_slots(plan, order, spans)

    half = heads * tok
    def parts_of(stats):
        return [stats[k * STAT_ROWS : (k + 1) * STAT_ROWS, :] for k in range(STATS)]

    def partner(x):
        return jnp.concatenate([x[heads : 2 * heads], x[:heads], x[2 * heads :]], axis=0)

    top_mine, sum_mine, delta_mine = parts_of(stats_own[...])
    top_other, sum_other, delta_other = [partner(x) for x in parts_of(stats_mate[...])]
    top = jnp.maximum(top_mine, top_other)
    f_mine, f_other = jnp.exp2(top_mine - top), jnp.exp2(top_other - top)
    total = sum_mine * f_mine + sum_other * f_other
    used = lax.broadcasted_iota(jnp.int32, total.shape, 0) < 2 * heads
    total = jnp.where(used, total, 1.0)
    scales = f_mine / total
    deltas = (delta_mine * f_mine + delta_other * f_other) / total * scales
    columns = columns_of(jnp.concatenate([scales, deltas], axis=0))
    for j in range(2 * heads):
        r = slice(j * tok, (j + 1) * tok)
        h = slice((j % heads) * dim, (j % heads + 1) * dim)
        scale = columns[:, j : j + 1]
        delta = columns[:, STAT_ROWS + j : STAT_ROWS + j + 1]
        delta_rows[r, :] = jnp.broadcast_to(delta, (tok, LANES))
        out = out_keep if j < heads else out_give
        g_rows[r, :] = (g_raw[r, :].astype(jnp.float32) * scale).astype(jnp.bfloat16)
        out[:, h] = (acc_in[r, :] * scale).astype(jnp.bfloat16)
    for j in range(2 * heads):
        r = slice(j * tok, (j + 1) * tok)
        g_cols[:, r] = jnp.transpose(g_rows[r, :])
    chunks = [slice(r, r + group) for r in range(0, 2 * half, group)]

    _, lower, own_span = unpack(plan, spans)

    @pl.loop(0, spans)
    def _(slot):
        span = plan[3 + 2 * spans + slot]

        @pl.when((span < lower) | (span > own_span))
        def _():
            dkv_keep[slot] = jnp.zeros(dkv_keep.shape[1:], dkv_keep.dtype)
            dkv_give[slot] = jnp.zeros(dkv_give.shape[1:], dkv_give.dtype)

    def grads_of(first, n):
        values = stacked(order, first, n, slice(dim, 2 * dim), kv_mine, kv_mate)
        for c in chunks:
            d_prob = lane_tiles(dot_rows(g_rows[c, :], values))
            delta = delta_rows[c, :]
            p = sum([lane_tiles(prob[first + k, c, :].astype(jnp.float32)) for k in range(n)], [])
            tiles = [x * (y - delta) for x, y in zip(p, d_prob)]
            per = len(tiles) // n
            for k in range(n):
                block = jnp.concatenate(tiles[k * per : (k + 1) * per], axis=1)
                ds_rows[first + k, c, :] = block.astype(jnp.bfloat16)
        for k in range(n):
            b = first + k
            pltpu.make_async_copy(ds_rows.at[b], ds_out.at[b], sems.at[b]).start()

    def keys_of(first, n):
        for k in range(n):
            slot = order[first + k]
            d_keys = jnp.transpose(dot(q_cols[...], ds_rows[first + k]) * LN2)
            d_keys = d_keys.astype(jnp.bfloat16)
            dkv_keep[slot, :, :dim] = d_keys[:tok]
            dkv_give[slot, :, :dim] = d_keys[tok:]
            d_values = jnp.transpose(dot(g_cols[...], prob[first + k])).astype(jnp.bfloat16)
            dkv_keep[slot, :, dim:] = d_values[:tok]
            dkv_give[slot, :, dim:] = d_values[tok:]

    by_pairs(count, grads_of)
    by_pairs(count, keys_of)

    @pl.loop(0, count)
    def _(b):
        pltpu.make_async_copy(ds_rows.at[b], ds_out.at[b], sems.at[b]).wait()


def finish(
    plan, ds_in, kv_mine, kv_mate, d_queries, order, ds_rows, acc, sems,
    *, tok, heads, dim, first_row,
):
    count, _ = visible_slots(plan, order, order.shape[0])
    n_rows = heads * tok

    def fetch(b):
        source = ds_in.at[b, pl.ds(first_row, n_rows)]
        return pltpu.make_async_copy(source, ds_rows.at[b], sems.at[b])

    @pl.loop(0, count)
    def _(b):
        fetch(b).start()

    acc[...] = jnp.zeros_like(acc)

    def add(first, n):
        keys = stacked(order, first, n, slice(0, dim), kv_mine, kv_mate)
        for k in range(n):
            fetch(first + k).wait()
        ds = jnp.concatenate([ds_rows[first + k] for k in range(n)], axis=1)
        acc[...] += dot(ds, keys)

    by_pairs(count, add)
    for h in range(heads):
        rows_of = acc[h * tok : (h + 1) * tok, :] / math.sqrt(dim)
        d_queries[:, h * dim : (h + 1) * dim] = rows_of.astype(jnp.bfloat16)


def spread(keys, values, queries, out, squares):
    both = jnp.concatenate([keys[...], values[...]], axis=1)
    for n in range(out.shape[0]):
        out[n] = both
    squares[...] = squares_of(queries[...])


SMEM_SPEC = pl.BlockSpec(memory_space=pltpu.SMEM)
HBM_SPEC = pl.BlockSpec(memory_space=pltpu.HBM)
VMEM_SPEC = pl.BlockSpec(memory_space=pltpu.VMEM)


def sizes_of(q_raw, kv_mine):
    n_rows, dim = q_raw.shape
    spans, tok, _ = kv_mine.shape
    return spans, tok, dim, n_rows // (2 * tok), n_rows


def small_params(limit=SMALL_LIMIT):
    return pltpu.CompilerParams(vmem_limit_bytes=limit)


def row_squares_call(own, q_mate):
    return pl.pallas_call(
        row_squares,
        out_shape=jax.ShapeDtypeStruct((2, own.shape[1]), jnp.float32),
        in_specs=[VMEM_SPEC] * 2,
        out_specs=VMEM_SPEC,
        compiler_params=small_params(),
        cost_estimate=LONG,
        name="row_squares",
    )(own, q_mate)


def normalize_call(square_sum, gain, q_raw, width):
    tok = square_sum.shape[1]
    n_rows, dim = q_raw.shape
    return pl.pallas_call(
        functools.partial(
            normalize, tok=tok, heads=n_rows // (2 * tok), dim=dim, width=width
        ),
        out_shape=(
            jax.ShapeDtypeStruct((n_rows, dim), jnp.bfloat16),
            jax.ShapeDtypeStruct((dim, n_rows), jnp.bfloat16),
        ),
        in_specs=[VMEM_SPEC] * 3,
        out_specs=(VMEM_SPEC,) * 2,
        compiler_params=small_params(),
        cost_estimate=SHORT,
        name="normalize",
    )(square_sum, gain, q_raw)


def prepare_call(queries, q_mate, out_grad, g_mate, dim):
    tok, local = queries.shape
    heads = local // dim
    rows = jax.ShapeDtypeStruct((2 * heads * tok, dim), jnp.bfloat16)
    return pl.pallas_call(
        functools.partial(prepare, tok=tok, heads=heads, dim=dim),
        out_shape=(rows, rows),
        in_specs=[VMEM_SPEC] * 4,
        out_specs=(VMEM_SPEC,) * 2,
        compiler_params=small_params(),
        cost_estimate=SHORT,
        name="prepare",
    )(queries, q_mate, out_grad, g_mate)


def add_pair(one, other, out):
    out[...] = (one[...].astype(jnp.float32) + other[...].astype(jnp.float32)).astype(out.dtype)


def add_pair_call(one, other):
    return pl.pallas_call(
        add_pair,
        out_shape=jax.ShapeDtypeStruct(one.shape, jnp.bfloat16),
        in_specs=[VMEM_SPEC] * 2,
        out_specs=VMEM_SPEC,
        compiler_params=small_params(),
        name="add_pair",
    )(one, other)


def merge_call(*parts):
    rows = jax.ShapeDtypeStruct(parts[0].shape, jnp.bfloat16)
    return pl.pallas_call(
        merge,
        out_shape=(rows, rows),
        in_specs=[VMEM_SPEC] * 4,
        out_specs=(VMEM_SPEC,) * 2,
        compiler_params=small_params(),
        cost_estimate=SHORT,
        name="merge",
    )(*parts)


def forward_call(plan, q_rows, g_raw, kv_mine, kv_mate, group=384):
    spans, tok, dim, heads, n_rows = sizes_of(q_rows, kv_mine)
    return pl.pallas_call(
        functools.partial(forward, tok=tok, heads=heads, dim=dim, group=group),
        out_shape=(
            jax.ShapeDtypeStruct((spans, n_rows, 2 * tok), jnp.bfloat16),
            jax.ShapeDtypeStruct((n_rows, dim), jnp.float32),
            jax.ShapeDtypeStruct((STATS * STAT_ROWS, LANES), jnp.float32),
        ),
        in_specs=[SMEM_SPEC] + [VMEM_SPEC] * 4,
        out_specs=(VMEM_SPEC,) * 3,
        scratch_shapes=[
            pltpu.SMEM((spans,), jnp.int32),
            pltpu.VMEM((spans, n_rows, 2 * tok), jnp.float32),
            pltpu.VMEM((n_rows, LANES), jnp.float32),
            pltpu.VMEM((n_rows, LANES), jnp.float32),
        ],
        compiler_params=pltpu.CompilerParams(vmem_limit_bytes=VMEM_LIMIT),
        name="attend_forward",
    )(plan, q_rows, g_raw, kv_mine, kv_mate)


def backward_call(
    plan, prob, stats_own, stats_mate, acc, q_cols, g_raw, kv_mine, kv_mate, group=768
):
    spans, tok, dim, heads, n_rows = sizes_of(g_raw, kv_mine)
    rows = jax.ShapeDtypeStruct((tok, heads * dim), jnp.bfloat16)
    part = jax.ShapeDtypeStruct(kv_mine.shape, jnp.bfloat16)
    return pl.pallas_call(
        functools.partial(backward, tok=tok, heads=heads, dim=dim, group=group),
        out_shape=(rows, rows, pltpu.HBM(prob.shape, jnp.bfloat16), part, part),
        in_specs=[SMEM_SPEC] + [VMEM_SPEC] * 8,
        out_specs=(VMEM_SPEC, VMEM_SPEC, HBM_SPEC, VMEM_SPEC, VMEM_SPEC),
        scratch_shapes=[
            pltpu.SMEM((spans,), jnp.int32),
            pltpu.VMEM((n_rows, dim), jnp.bfloat16),
            pltpu.VMEM(prob.shape, jnp.bfloat16),
            pltpu.VMEM((n_rows, LANES), jnp.float32),
            pltpu.VMEM((dim, n_rows), jnp.bfloat16),
            pltpu.SemaphoreType.DMA((spans,)),
        ],
        compiler_params=small_params(BACKWARD_LIMIT),
        name="attend_backward",
    )(plan, prob, stats_own, stats_mate, acc, q_cols, g_raw, kv_mine, kv_mate)


def finish_call(plan, ds_rows, kv_mine, kv_mate, side, cost):
    ds_rows = pltpu.with_memory_space_constraint(ds_rows, pltpu.HBM)
    spans, n_rows, n_keys = ds_rows.shape
    _, tok, both = kv_mine.shape
    dim = both // 2
    half = n_rows // 2
    heads = half // tok
    return pl.pallas_call(
        functools.partial(finish, tok=tok, heads=heads, dim=dim, first_row=side * half),
        out_shape=jax.ShapeDtypeStruct((tok, heads * dim), jnp.bfloat16),
        in_specs=[SMEM_SPEC, HBM_SPEC, VMEM_SPEC, VMEM_SPEC],
        out_specs=VMEM_SPEC,
        scratch_shapes=[
            pltpu.SMEM((spans,), jnp.int32),
            pltpu.VMEM((spans, half, n_keys), jnp.bfloat16),
            pltpu.VMEM((half, dim), jnp.float32),
            pltpu.SemaphoreType.DMA((spans,)),
        ],
        compiler_params=small_params(),
        cost_estimate=cost,
        name=("finish_own", "finish_mate")[side],
    )(plan, ds_rows, kv_mine, kv_mate)


def spread_call(keys, values, queries, n_z):
    tok, dim = keys.shape
    return pl.pallas_call(
        spread,
        out_shape=(
            jax.ShapeDtypeStruct((n_z, tok, 2 * dim), jnp.bfloat16),
            jax.ShapeDtypeStruct((1, tok), jnp.float32),
        ),
        in_specs=[VMEM_SPEC] * 3,
        out_specs=(VMEM_SPEC,) * 2,
        name="spread",
    )(keys, values, queries)


def head_sum(x):
    x = x + lax.ppermute(x, "xl", SWAP)
    n = lax.axis_size("y")
    others = [lax.ppermute(x, "y", [(i, (i + d) % n) for i in range(n)]) for d in range(1, n)]
    return functools.reduce(jnp.add, others, x)


def shards(
    queries, key_states, value_states, out_grad, norm_gain, mask_kind, range_start, placement
):
    tok, local = queries.shape
    dim = key_states.shape[1]
    n_heads = lax.axis_size(HEAD)
    n_z = lax.axis_size("z")
    places = [lax.axis_index(a).astype(jnp.int32)[None] for a in CTX]
    plan = jnp.concatenate(places + [mask_kind, range_start, placement])

    q_mate = lax.ppermute(queries, "xh", SWAP)
    g_mate = lax.ppermute(out_grad, "xh", SWAP)
    kv_out, own_squares = spread_call(key_states, value_states, queries, n_z)
    kv_mine = lax.all_to_all(kv_out, "z", 0, 0)
    square_sum = head_sum(row_squares_call(own_squares, q_mate))
    q_raw, g_raw = prepare_call(queries, q_mate, out_grad, g_mate, dim)
    kv_mine, square_sum, q_raw, g_raw = lax.optimization_barrier(
        (kv_mine, square_sum, q_raw, g_raw)
    )
    kv_mate = lax.ppermute(kv_mine, "core", SWAP)

    q_rows, q_cols = normalize_call(square_sum, norm_gain[None, :], q_raw, local * n_heads)
    prob, acc, stats = forward_call(plan, q_rows, g_raw, kv_mine, kv_mate)
    stats_mate = lax.ppermute(stats, "xh", SWAP)
    out_keep, out_give, ds_rows, dkv_keep, dkv_give = backward_call(
        plan, prob, stats, stats_mate, acc, q_cols, g_raw, kv_mine, kv_mate
    )
    out_got = lax.ppermute(out_give, "xh", SWAP)
    dkv_got = lax.ppermute(dkv_give, "core", SWAP)
    chip = add_pair_call(dkv_keep, dkv_got)
    chip, ds_rows = lax.optimization_barrier((chip, ds_rows))
    pieces = lax.all_to_all(chip, "z", 0, 0)
    dq_give = finish_call(plan, ds_rows, kv_mine, kv_mate, 1, MEDIUM)
    dq_got = lax.ppermute(dq_give, "xh", SWAP)
    ds_rows, _ = lax.optimization_barrier((ds_rows, dq_give))
    dq_keep = finish_call(plan, ds_rows, kv_mine, kv_mate, 0, MEDIUM)
    attn_out, d_queries = merge_call(out_keep, out_got, dq_keep, dq_got)
    total = jnp.sum(pieces.astype(jnp.float32), axis=0).astype(jnp.bfloat16)
    return (attn_out, d_queries, total[:, :dim], total[:, dim:])


def solution(mesh):
    fine = Mesh(mesh.devices.reshape(8, 2, 2, 4, 2), ("z", "xh", "core", "y", "xl"))
    rows = P(CTX, HEAD)
    in_specs = (rows, rows, rows, rows, P(HEAD), P(), P(), P())
    out_specs = (rows, rows, rows, rows)
    return jax.shard_map(shards, mesh=fine, in_specs=in_specs, out_specs=out_specs, check_vma=False)
```

```python
import functools
import math

import jax
import jax.numpy as jnp
from jax import lax
from jax.experimental import pallas as pl
from jax.experimental.pallas import tpu as pltpu
from jax.sharding import Mesh
from jax.sharding import PartitionSpec as P

NEG = -1e30
EPS = 1e-06
LOG2E = 1.4426950408889634
LN2 = 0.6931471805599453
LANES = 128
STATS = 3
STAT_ROWS = 16

CTX = ("z", "xh", "core")
HEAD = ("y", "xl")
SWAP = [(0, 1), (1, 0)]
VMEM_LIMIT = 24 * 2**20
BACKWARD_LIMIT = 18 * 2**20
SMALL_LIMIT = 9 * 2**20
LONG = pl.CostEstimate(flops=2 * 10**10, bytes_accessed=2**20, transcendentals=0)
MEDIUM = pl.CostEstimate(flops=3 * 10**9, bytes_accessed=2**10, transcendentals=0)
SHORT = pl.CostEstimate(flops=2**10, bytes_accessed=2**10, transcendentals=0)


def dot_rows(left_side, right_side):
    return lax.dot_general(
        left_side, right_side, (((1,), (1,)), ((), ())), preferred_element_type=jnp.float32
    )


def dot_cols(left_side, right_side):
    return lax.dot_general(
        left_side, right_side, (((0,), (0,)), ((), ())), preferred_element_type=jnp.float32
    )


def dot(left_side, right_side):
    return jnp.dot(left_side, right_side, preferred_element_type=jnp.float32)


def lane_tiles(x):
    return [x[:, j : j + LANES] for j in range(0, x.shape[1], LANES)]


def lane_sum(x):
    return jnp.sum(x, axis=1, keepdims=True)


def unpack(plan, spans):
    own_span = plan[3 + 2 * spans + plan[0]]
    lower = plan[3 + spans + own_span]
    return own_span - lower + 1, lower, own_span


def visible_slots(plan, order, spans):
    count, lower, own_span = unpack(plan, spans)

    @pl.loop(0, spans)
    def _(slot):
        span = plan[3 + 2 * spans + slot]

        @pl.when((lower <= span) & (span < own_span))
        def _():
            order[span - lower + 1] = slot

    order[0] = plan[0]

    return count, own_span


def stacked(order, first, n, lanes, kv_mine, kv_mate):
    parts = []
    for k in range(n):
        slot = order[first + k]
        parts += [kv_mine[slot, :, lanes], kv_mate[slot, :, lanes]]
    return jnp.concatenate(parts, axis=0)


def by_pairs(count, body):
    @pl.loop(0, count // 2)
    def _(i):
        body(2 * i, 2)

    @pl.when(count % 2 == 1)
    def _():
        body(count - 1, 1)


def columns_of(table):
    pad = jnp.zeros((LANES - table.shape[0], LANES), jnp.float32)
    return jnp.transpose(jnp.concatenate([table, pad], axis=0))


def squares_of(rows_of):
    wide = rows_of.astype(jnp.float32)
    total = functools.reduce(jnp.add, lane_tiles(wide * wide))
    return jnp.sum(jnp.transpose(total), axis=0, keepdims=True)


def row_squares(own, q_mate, parts):
    parts[0:1, :] = own[...]
    parts[1:2, :] = squares_of(q_mate[...])


def normalize(square_sum, gain, q_raw, q_rows, q_cols, *, tok, heads, dim, width):
    sums = columns_of(square_sum[...])
    scale = lax.rsqrt(sums / width + EPS) * (LOG2E / math.sqrt(dim))
    for side in range(2):
        for h in range(heads):
            r = slice((side * heads + h) * tok, (side * heads + h + 1) * tok)
            normed = q_raw[r, :].astype(jnp.float32) * scale[:, side : side + 1]
            normed = (normed * gain[:, h * dim : (h + 1) * dim]).astype(jnp.bfloat16)
            q_rows[r, :] = normed
            q_cols[:, r] = jnp.transpose(normed)


def prepare(queries, q_mate, out_grad, g_mate, q_raw, g_raw, *, tok, heads, dim):
    for side, (q_part, g_part) in enumerate(((queries, out_grad), (q_mate, g_mate))):
        for h in range(heads):
            first = (side * heads + h) * tok
            q_raw[first : first + tok, :] = q_part[:, h * dim : (h + 1) * dim]
            g_raw[first : first + tok, :] = g_part[:, h * dim : (h + 1) * dim]


def merge(out_keep, out_got, dq_keep, dq_got, out, dq):
    out[...] = (out_keep[...].astype(jnp.float32) + out_got[...].astype(jnp.float32)).astype(out.dtype)
    dq[...] = (dq_keep[...].astype(jnp.float32) + dq_got[...].astype(jnp.float32)).astype(dq.dtype)


def forward(
    plan, q_rows, g_raw, kv_mine, kv_mate,
    prob, acc, stats,
    order, score, row_max, row_sum,
    *, tok, heads, dim, group,
):
    spans = order.shape[0]
    half = heads * tok
    keys_n = 2 * tok
    count, own_span = visible_slots(plan, order, spans)
    chunks = [slice(r, r + group) for r in range(0, 2 * half, group)]

    def score_own():
        keys = stacked(order, 0, 1, slice(0, dim), kv_mine, kv_mate)
        free = plan[3 + own_span] == 0
        q_t = lax.broadcasted_iota(jnp.int32, (group, keys_n), 0) % tok
        k_t = lax.broadcasted_iota(jnp.int32, (group, keys_n), 1)
        core = plan[2]
        k_pos = plan[1] * keys_n + jnp.where(
            k_t < tok, core * tok + k_t, (1 - core) * tok + k_t - tok
        )
        for c in chunks:
            q_xh = plan[1] if c.start < half else 1 - plan[1]
            q_pos = (q_xh * 2 + core) * tok + q_t
            s = dot_rows(q_rows[c, :], keys)
            s = jnp.where((k_pos <= q_pos) | free, s, NEG)
            score[0, c, :] = s
            row_max[c, :] = functools.reduce(jnp.maximum, lane_tiles(s))

    score_own()

    def score_blocks(first, n):
        keys = stacked(order, first, n, slice(0, dim), kv_mine, kv_mate)
        for c in chunks:
            s = dot_rows(q_rows[c, :], keys)
            for k in range(n):
                score[first + k, c, :] = s[:, k * keys_n : (k + 1) * keys_n]
            row_max[c, :] = functools.reduce(jnp.maximum, lane_tiles(s), row_max[c, :])

    by_pairs(count - 1, lambda first, n: score_blocks(first + 1, n))

    for c in chunks:
        top = jnp.max(row_max[c, :], axis=1, keepdims=True)
        row_max[c, :] = jnp.broadcast_to(top, (group, LANES))

    def weigh(first, n, start):
        values = stacked(order, first, n, slice(dim, 2 * dim), kv_mine, kv_mate)
        for c in chunks:
            top = row_max[c, :]
            blocks = [lane_tiles(score[first + k, c, :]) for k in range(n)]
            tiles = [[jnp.exp2(t - top) for t in b] for b in blocks]
            sums = functools.reduce(jnp.add, sum(tiles, []))
            row_sum[c, :] = sums if start else row_sum[c, :] + sums
            p = [jnp.concatenate(b, axis=1).astype(jnp.bfloat16) for b in tiles]
            for k in range(n):
                prob[first + k, c, :] = p[k]
            mixed = dot(jnp.concatenate(p, axis=1), values)
            acc[c, :] = mixed if start else acc[c, :] + mixed

    odd = count % 2

    @pl.when(odd == 1)
    def _():
        weigh(0, 1, True)

    @pl.when(odd == 0)
    def _():
        weigh(0, 2, True)

    @pl.loop(0, (count - 1) // 2)
    def _(i):
        weigh(2 * i + 2 - odd, 2, False)

    lane = lax.broadcasted_iota(jnp.int32, (tok, LANES), 1)
    table = jnp.zeros((tok, LANES), jnp.float32)
    for j in range(2 * heads):
        r = slice(j * tok, (j + 1) * tok)
        grad = g_raw[r, :].astype(jnp.float32)
        columns = (row_max[r, :], lane_sum(row_sum[r, :]), lane_sum(grad * acc[r, :]))
        for k, column in enumerate(columns):
            table = jnp.where(lane == STAT_ROWS * k + j, column, table)
    stats[...] = jnp.transpose(table)[: stats.shape[0], :]


def backward(
    plan, prob, stats_own, stats_mate, acc_in, q_cols, g_raw, kv_mine, kv_mate,
    out_keep, out_give, ds_out, dkv_keep, dkv_give,
    order, g_rows, ds_rows, delta_rows, g_cols, sems,
    *, tok, heads, dim, group,
):
    spans = order.shape[0]
    count, _ = visible_slots(plan, order, spans)

    half = heads * tok
    def parts_of(stats):
        return [stats[k * STAT_ROWS : (k + 1) * STAT_ROWS, :] for k in range(STATS)]

    def partner(x):
        return jnp.concatenate([x[heads : 2 * heads], x[:heads], x[2 * heads :]], axis=0)

    top_mine, sum_mine, delta_mine = parts_of(stats_own[...])
    top_other, sum_other, delta_other = [partner(x) for x in parts_of(stats_mate[...])]
    top = jnp.maximum(top_mine, top_other)
    f_mine, f_other = jnp.exp2(top_mine - top), jnp.exp2(top_other - top)
    total = sum_mine * f_mine + sum_other * f_other
    used = lax.broadcasted_iota(jnp.int32, total.shape, 0) < 2 * heads
    total = jnp.where(used, total, 1.0)
    scales = f_mine / total
    deltas = (delta_mine * f_mine + delta_other * f_other) / total * scales
    columns = columns_of(jnp.concatenate([scales, deltas], axis=0))
    for j in range(2 * heads):
        r = slice(j * tok, (j + 1) * tok)
        h = slice((j % heads) * dim, (j % heads + 1) * dim)
        scale = columns[:, j : j + 1]
        delta = columns[:, STAT_ROWS + j : STAT_ROWS + j + 1]
        delta_rows[r, :] = jnp.broadcast_to(delta, (tok, LANES))
        out = out_keep if j < heads else out_give
        g_rows[r, :] = (g_raw[r, :].astype(jnp.float32) * scale).astype(jnp.bfloat16)
        out[:, h] = (acc_in[r, :] * scale).astype(jnp.bfloat16)
    for j in range(2 * heads):
        r = slice(j * tok, (j + 1) * tok)
        g_cols[:, r] = jnp.transpose(g_rows[r, :])
    chunks = [slice(r, r + group) for r in range(0, 2 * half, group)]

    _, lower, own_span = unpack(plan, spans)

    @pl.loop(0, spans)
    def _(slot):
        span = plan[3 + 2 * spans + slot]

        @pl.when((span < lower) | (span > own_span))
        def _():
            dkv_keep[slot] = jnp.zeros(dkv_keep.shape[1:], dkv_keep.dtype)
            dkv_give[slot] = jnp.zeros(dkv_give.shape[1:], dkv_give.dtype)

    def grads_of(first, n):
        values = stacked(order, first, n, slice(dim, 2 * dim), kv_mine, kv_mate)
        for c in chunks:
            d_prob = lane_tiles(dot_rows(g_rows[c, :], values))
            delta = delta_rows[c, :]
            p = sum([lane_tiles(prob[first + k, c, :].astype(jnp.float32)) for k in range(n)], [])
            tiles = [x * (y - delta) for x, y in zip(p, d_prob)]
            per = len(tiles) // n
            for k in range(n):
                block = jnp.concatenate(tiles[k * per : (k + 1) * per], axis=1)
                ds_rows[first + k, c, :] = block.astype(jnp.bfloat16)
        for k in range(n):
            b = first + k
            pltpu.make_async_copy(ds_rows.at[b], ds_out.at[b], sems.at[b]).start()

    def keys_of(first, n):
        for k in range(n):
            slot = order[first + k]
            d_keys = jnp.transpose(dot(q_cols[...], ds_rows[first + k]) * LN2)
            d_keys = d_keys.astype(jnp.bfloat16)
            dkv_keep[slot, :, :dim] = d_keys[:tok]
            dkv_give[slot, :, :dim] = d_keys[tok:]
            d_values = jnp.transpose(dot(g_cols[...], prob[first + k])).astype(jnp.bfloat16)
            dkv_keep[slot, :, dim:] = d_values[:tok]
            dkv_give[slot, :, dim:] = d_values[tok:]

    by_pairs(count, grads_of)
    by_pairs(count, keys_of)

    @pl.loop(0, count)
    def _(b):
        pltpu.make_async_copy(ds_rows.at[b], ds_out.at[b], sems.at[b]).wait()


def finish(
    plan, ds_in, kv_mine, kv_mate, d_queries, order, ds_rows, acc, sems,
    *, tok, heads, dim, first_row,
):
    count, _ = visible_slots(plan, order, order.shape[0])
    n_rows = heads * tok

    def fetch(b):
        source = ds_in.at[b, pl.ds(first_row, n_rows)]
        return pltpu.make_async_copy(source, ds_rows.at[b], sems.at[b])

    @pl.loop(0, count)
    def _(b):
        fetch(b).start()

    acc[...] = jnp.zeros_like(acc)

    def add(first, n):
        keys = stacked(order, first, n, slice(0, dim), kv_mine, kv_mate)
        for k in range(n):
            fetch(first + k).wait()
        ds = jnp.concatenate([ds_rows[first + k] for k in range(n)], axis=1)
        acc[...] += dot(ds, keys)

    by_pairs(count, add)
    for h in range(heads):
        rows_of = acc[h * tok : (h + 1) * tok, :] / math.sqrt(dim)
        d_queries[:, h * dim : (h + 1) * dim] = rows_of.astype(jnp.bfloat16)


def spread(keys_in, values_in, queries_in, out, squares, keys, values, queries, sems):
    moved = [
        pltpu.make_async_copy(source, target, sems.at[n])
        for n, (source, target) in enumerate(
            ((keys_in, keys), (values_in, values), (queries_in, queries))
        )
    ]
    for copy in moved:
        copy.start()
    moved[0].wait()
    moved[1].wait()
    both = jnp.concatenate([keys[...], values[...]], axis=1)
    for n in range(out.shape[0]):
        out[n] = both
    moved[2].wait()
    squares[...] = squares_of(queries[...])


SMEM_SPEC = pl.BlockSpec(memory_space=pltpu.SMEM)
HBM_SPEC = pl.BlockSpec(memory_space=pltpu.HBM)
VMEM_SPEC = pl.BlockSpec(memory_space=pltpu.VMEM)


def sizes_of(q_raw, kv_mine):
    n_rows, dim = q_raw.shape
    spans, tok, _ = kv_mine.shape
    return spans, tok, dim, n_rows // (2 * tok), n_rows


def small_params(limit=SMALL_LIMIT):
    return pltpu.CompilerParams(vmem_limit_bytes=limit)


def row_squares_call(own, q_mate):
    return pl.pallas_call(
        row_squares,
        out_shape=jax.ShapeDtypeStruct((2, own.shape[1]), jnp.float32),
        in_specs=[VMEM_SPEC] * 2,
        out_specs=VMEM_SPEC,
        compiler_params=small_params(),
        cost_estimate=LONG,
        name="row_squares",
    )(own, q_mate)


def normalize_call(square_sum, gain, q_raw, width):
    tok = square_sum.shape[1]
    n_rows, dim = q_raw.shape
    return pl.pallas_call(
        functools.partial(
            normalize, tok=tok, heads=n_rows // (2 * tok), dim=dim, width=width
        ),
        out_shape=(
            jax.ShapeDtypeStruct((n_rows, dim), jnp.bfloat16),
            jax.ShapeDtypeStruct((dim, n_rows), jnp.bfloat16),
        ),
        in_specs=[VMEM_SPEC] * 3,
        out_specs=(VMEM_SPEC,) * 2,
        compiler_params=small_params(),
        cost_estimate=SHORT,
        name="normalize",
    )(square_sum, gain, q_raw)


def prepare_call(queries, q_mate, out_grad, g_mate, dim):
    tok, local = queries.shape
    heads = local // dim
    rows = jax.ShapeDtypeStruct((2 * heads * tok, dim), jnp.bfloat16)
    return pl.pallas_call(
        functools.partial(prepare, tok=tok, heads=heads, dim=dim),
        out_shape=(rows, rows),
        in_specs=[VMEM_SPEC] * 4,
        out_specs=(VMEM_SPEC,) * 2,
        compiler_params=small_params(),
        cost_estimate=SHORT,
        name="prepare",
    )(queries, q_mate, out_grad, g_mate)


def add_pair(one, other, out):
    out[...] = (one[...].astype(jnp.float32) + other[...].astype(jnp.float32)).astype(out.dtype)


def add_pair_call(one, other):
    return pl.pallas_call(
        add_pair,
        out_shape=jax.ShapeDtypeStruct(one.shape, jnp.bfloat16),
        in_specs=[VMEM_SPEC] * 2,
        out_specs=VMEM_SPEC,
        compiler_params=small_params(),
        name="add_pair",
    )(one, other)


def merge_call(*parts):
    rows = jax.ShapeDtypeStruct(parts[0].shape, jnp.bfloat16)
    return pl.pallas_call(
        merge,
        out_shape=(rows, rows),
        in_specs=[VMEM_SPEC] * 4,
        out_specs=(VMEM_SPEC,) * 2,
        compiler_params=small_params(),
        cost_estimate=SHORT,
        name="merge",
    )(*parts)


def forward_call(plan, q_rows, g_raw, kv_mine, kv_mate, group=384):
    spans, tok, dim, heads, n_rows = sizes_of(q_rows, kv_mine)
    return pl.pallas_call(
        functools.partial(forward, tok=tok, heads=heads, dim=dim, group=group),
        out_shape=(
            jax.ShapeDtypeStruct((spans, n_rows, 2 * tok), jnp.bfloat16),
            jax.ShapeDtypeStruct((n_rows, dim), jnp.float32),
            jax.ShapeDtypeStruct((STATS * STAT_ROWS, LANES), jnp.float32),
        ),
        in_specs=[SMEM_SPEC] + [VMEM_SPEC] * 4,
        out_specs=(VMEM_SPEC,) * 3,
        scratch_shapes=[
            pltpu.SMEM((spans,), jnp.int32),
            pltpu.VMEM((spans, n_rows, 2 * tok), jnp.float32),
            pltpu.VMEM((n_rows, LANES), jnp.float32),
            pltpu.VMEM((n_rows, LANES), jnp.float32),
        ],
        compiler_params=pltpu.CompilerParams(vmem_limit_bytes=VMEM_LIMIT),
        name="attend_forward",
    )(plan, q_rows, g_raw, kv_mine, kv_mate)


def backward_call(
    plan, prob, stats_own, stats_mate, acc, q_cols, g_raw, kv_mine, kv_mate, group=768
):
    spans, tok, dim, heads, n_rows = sizes_of(g_raw, kv_mine)
    rows = jax.ShapeDtypeStruct((tok, heads * dim), jnp.bfloat16)
    part = jax.ShapeDtypeStruct(kv_mine.shape, jnp.bfloat16)
    return pl.pallas_call(
        functools.partial(backward, tok=tok, heads=heads, dim=dim, group=group),
        out_shape=(rows, rows, pltpu.HBM(prob.shape, jnp.bfloat16), part, part),
        in_specs=[SMEM_SPEC] + [VMEM_SPEC] * 8,
        out_specs=(VMEM_SPEC, VMEM_SPEC, HBM_SPEC, VMEM_SPEC, VMEM_SPEC),
        scratch_shapes=[
            pltpu.SMEM((spans,), jnp.int32),
            pltpu.VMEM((n_rows, dim), jnp.bfloat16),
            pltpu.VMEM(prob.shape, jnp.bfloat16),
            pltpu.VMEM((n_rows, LANES), jnp.float32),
            pltpu.VMEM((dim, n_rows), jnp.bfloat16),
            pltpu.SemaphoreType.DMA((spans,)),
        ],
        compiler_params=small_params(BACKWARD_LIMIT),
        name="attend_backward",
    )(plan, prob, stats_own, stats_mate, acc, q_cols, g_raw, kv_mine, kv_mate)


def finish_call(plan, ds_rows, kv_mine, kv_mate, side, cost):
    ds_rows = pltpu.with_memory_space_constraint(ds_rows, pltpu.HBM)
    spans, n_rows, n_keys = ds_rows.shape
    _, tok, both = kv_mine.shape
    dim = both // 2
    half = n_rows // 2
    heads = half // tok
    return pl.pallas_call(
        functools.partial(finish, tok=tok, heads=heads, dim=dim, first_row=side * half),
        out_shape=jax.ShapeDtypeStruct((tok, heads * dim), jnp.bfloat16),
        in_specs=[SMEM_SPEC, HBM_SPEC, VMEM_SPEC, VMEM_SPEC],
        out_specs=VMEM_SPEC,
        scratch_shapes=[
            pltpu.SMEM((spans,), jnp.int32),
            pltpu.VMEM((spans, half, n_keys), jnp.bfloat16),
            pltpu.VMEM((half, dim), jnp.float32),
            pltpu.SemaphoreType.DMA((spans,)),
        ],
        compiler_params=small_params(),
        cost_estimate=cost,
        name=("finish_own", "finish_mate")[side],
    )(plan, ds_rows, kv_mine, kv_mate)


def spread_call(keys, values, queries, n_z):
    tok, dim = keys.shape
    arrays = [pltpu.with_memory_space_constraint(x, pltpu.HBM) for x in (keys, values, queries)]
    return pl.pallas_call(
        spread,
        out_shape=(
            jax.ShapeDtypeStruct((n_z, tok, 2 * dim), jnp.bfloat16),
            jax.ShapeDtypeStruct((1, tok), jnp.float32),
        ),
        in_specs=[HBM_SPEC] * 3,
        out_specs=(VMEM_SPEC,) * 2,
        scratch_shapes=[pltpu.VMEM(x.shape, x.dtype) for x in (keys, values, queries)]
        + [pltpu.SemaphoreType.DMA((3,))],
        compiler_params=small_params(),
        name="spread",
    )(*arrays)


def head_sum(x):
    x = x + lax.ppermute(x, "xl", SWAP)
    n = lax.axis_size("y")
    others = [lax.ppermute(x, "y", [(i, (i + d) % n) for i in range(n)]) for d in range(1, n)]
    return functools.reduce(jnp.add, others, x)


def shards(
    queries, key_states, value_states, out_grad, norm_gain, mask_kind, range_start, placement
):
    tok, local = queries.shape
    dim = key_states.shape[1]
    n_heads = lax.axis_size(HEAD)
    n_z = lax.axis_size("z")
    places = [lax.axis_index(a).astype(jnp.int32)[None] for a in CTX]
    plan = jnp.concatenate(places + [mask_kind, range_start, placement])

    q_mate = lax.ppermute(queries, "xh", SWAP)
    g_mate = lax.ppermute(out_grad, "xh", SWAP)
    kv_out, own_squares = spread_call(key_states, value_states, queries, n_z)
    kv_mine = lax.all_to_all(kv_out, "z", 0, 0)
    square_sum = head_sum(row_squares_call(own_squares, q_mate))
    q_raw, g_raw = prepare_call(queries, q_mate, out_grad, g_mate, dim)
    kv_mine, square_sum, q_raw, g_raw = lax.optimization_barrier(
        (kv_mine, square_sum, q_raw, g_raw)
    )
    kv_mate = lax.ppermute(kv_mine, "core", SWAP)

    q_rows, q_cols = normalize_call(square_sum, norm_gain[None, :], q_raw, local * n_heads)
    prob, acc, stats = forward_call(plan, q_rows, g_raw, kv_mine, kv_mate)
    stats_mate = lax.ppermute(stats, "xh", SWAP)
    out_keep, out_give, ds_rows, dkv_keep, dkv_give = backward_call(
        plan, prob, stats, stats_mate, acc, q_cols, g_raw, kv_mine, kv_mate
    )
    out_got = lax.ppermute(out_give, "xh", SWAP)
    dkv_got = lax.ppermute(dkv_give, "core", SWAP)
    chip = add_pair_call(dkv_keep, dkv_got)
    chip, ds_rows = lax.optimization_barrier((chip, ds_rows))
    pieces = lax.all_to_all(chip, "z", 0, 0)
    dq_give = finish_call(plan, ds_rows, kv_mine, kv_mate, 1, MEDIUM)
    dq_got = lax.ppermute(dq_give, "xh", SWAP)
    ds_rows, _ = lax.optimization_barrier((ds_rows, dq_give))
    dq_keep = finish_call(plan, ds_rows, kv_mine, kv_mate, 0, MEDIUM)
    attn_out, d_queries = merge_call(out_keep, out_got, dq_keep, dq_got)
    total = jnp.sum(pieces.astype(jnp.float32), axis=0).astype(jnp.bfloat16)
    return (attn_out, d_queries, total[:, :dim], total[:, dim:])


def solution(mesh):
    fine = Mesh(mesh.devices.reshape(8, 2, 2, 4, 2), ("z", "xh", "core", "y", "xl"))
    rows = P(CTX, HEAD)
    in_specs = (rows, rows, rows, rows, P(HEAD), P(), P(), P())
    out_specs = (rows, rows, rows, rows)
    return jax.shard_map(shards, mesh=fine, in_specs=in_specs, out_specs=out_specs, check_vma=False)
```

```python
import functools
import math

import jax
import jax.numpy as jnp
from jax import lax
from jax.experimental import pallas as pl
from jax.experimental.pallas import tpu as pltpu
from jax.sharding import Mesh
from jax.sharding import PartitionSpec as P

NEG = -1e30
EPS = 1e-06
LOG2E = 1.4426950408889634
LN2 = 0.6931471805599453
LANES = 128
STATS = 3
STAT_ROWS = 16

CTX = ("z", "xh", "core")
HEAD = ("y", "xl")
SWAP = [(0, 1), (1, 0)]
VMEM_LIMIT = 24 * 2**20
BACKWARD_LIMIT = 18 * 2**20
SMALL_LIMIT = 9 * 2**20
LONG = pl.CostEstimate(flops=2 * 10**10, bytes_accessed=2**20, transcendentals=0)
MEDIUM = pl.CostEstimate(flops=3 * 10**9, bytes_accessed=2**10, transcendentals=0)
SHORT = pl.CostEstimate(flops=2**10, bytes_accessed=2**10, transcendentals=0)


def dot_rows(left_side, right_side):
    return lax.dot_general(
        left_side, right_side, (((1,), (1,)), ((), ())), preferred_element_type=jnp.float32
    )


def dot_cols(left_side, right_side):
    return lax.dot_general(
        left_side, right_side, (((0,), (0,)), ((), ())), preferred_element_type=jnp.float32
    )


def dot(left_side, right_side):
    return jnp.dot(left_side, right_side, preferred_element_type=jnp.float32)


def lane_tiles(x):
    return [x[:, j : j + LANES] for j in range(0, x.shape[1], LANES)]


def lane_sum(x):
    return jnp.sum(x, axis=1, keepdims=True)


def unpack(plan, spans):
    own_span = plan[3 + 2 * spans + plan[0]]
    lower = plan[3 + spans + own_span]
    return own_span - lower + 1, lower, own_span


def visible_slots(plan, order, spans):
    count, lower, own_span = unpack(plan, spans)

    @pl.loop(0, spans)
    def _(slot):
        span = plan[3 + 2 * spans + slot]

        @pl.when((lower <= span) & (span < own_span))
        def _():
            order[span - lower + 1] = slot

    order[0] = plan[0]

    return count, own_span


def stacked(order, first, n, lanes, kv_mine, kv_mate):
    parts = []
    for k in range(n):
        slot = order[first + k]
        parts += [kv_mine[slot, :, lanes], kv_mate[slot, :, lanes]]
    return jnp.concatenate(parts, axis=0)


def by_pairs(count, body):
    @pl.loop(0, count // 2)
    def _(i):
        body(2 * i, 2)

    @pl.when(count % 2 == 1)
    def _():
        body(count - 1, 1)


def columns_of(table):
    pad = jnp.zeros((LANES - table.shape[0], LANES), jnp.float32)
    return jnp.transpose(jnp.concatenate([table, pad], axis=0))


def squares_of(rows_of):
    wide = rows_of.astype(jnp.float32)
    total = functools.reduce(jnp.add, lane_tiles(wide * wide))
    return jnp.sum(jnp.transpose(total), axis=0, keepdims=True)


def row_squares(own, q_mate, parts):
    parts[0:1, :] = own[...]
    parts[1:2, :] = squares_of(q_mate[...])


def normalize(square_sum, gain, q_raw, q_rows, q_cols, *, tok, heads, dim, width):
    sums = columns_of(square_sum[...])
    scale = lax.rsqrt(sums / width + EPS) * (LOG2E / math.sqrt(dim))
    for side in range(2):
        for h in range(heads):
            r = slice((side * heads + h) * tok, (side * heads + h + 1) * tok)
            normed = q_raw[r, :].astype(jnp.float32) * scale[:, side : side + 1]
            normed = (normed * gain[:, h * dim : (h + 1) * dim]).astype(jnp.bfloat16)
            q_rows[r, :] = normed
            q_cols[:, r] = jnp.transpose(normed)


def prepare(queries, q_mate, out_grad, g_mate, q_raw, g_raw, g_turned, *, tok, heads, dim):
    for side, (q_part, g_part) in enumerate(((queries, out_grad), (q_mate, g_mate))):
        for h in range(heads):
            first = (side * heads + h) * tok
            q_raw[first : first + tok, :] = q_part[:, h * dim : (h + 1) * dim]
            g_head = g_part[:, h * dim : (h + 1) * dim]
            g_raw[first : first + tok, :] = g_head
            g_turned[:, first : first + tok] = jnp.transpose(g_head)


def merge(out_keep, out_got, dq_keep, dq_got, out, dq):
    out[...] = (out_keep[...].astype(jnp.float32) + out_got[...].astype(jnp.float32)).astype(out.dtype)
    dq[...] = (dq_keep[...].astype(jnp.float32) + dq_got[...].astype(jnp.float32)).astype(dq.dtype)


def forward(
    plan, q_rows, g_raw, kv_mine, kv_mate,
    prob, acc, stats,
    order, score, row_max, row_sum,
    *, tok, heads, dim, group,
):
    spans = order.shape[0]
    half = heads * tok
    keys_n = 2 * tok
    count, own_span = visible_slots(plan, order, spans)
    row_max[...] = jnp.full_like(row_max, NEG)
    row_sum[...] = jnp.zeros_like(row_sum)
    acc[...] = jnp.zeros_like(acc)
    chunks = [slice(r, r + group) for r in range(0, 2 * half, group)]

    def score_block(i, masked):
        slot = order[i]
        keys = jnp.concatenate([kv_mine[slot, :, :dim], kv_mate[slot, :, :dim]], axis=0)
        if masked:
            free = plan[3 + own_span] == 0
            q_t = lax.broadcasted_iota(jnp.int32, (group, keys_n), 0) % tok
            k_t = lax.broadcasted_iota(jnp.int32, (group, keys_n), 1)
            core = plan[2]
            k_pos = plan[1] * keys_n + jnp.where(
                k_t < tok, core * tok + k_t, (1 - core) * tok + k_t - tok
            )
        for c in chunks:
            s = dot_rows(q_rows[c, :], keys)
            if masked:
                q_xh = plan[1] if c.start < half else 1 - plan[1]
                q_pos = (q_xh * 2 + core) * tok + q_t
                s = jnp.where((k_pos <= q_pos) | free, s, NEG)
            score[i, c, :] = s
            row_max[c, :] = functools.reduce(jnp.maximum, lane_tiles(s), row_max[c, :])

    score_block(0, True)

    def score_blocks(first, n):
        keys = stacked(order, first, n, slice(0, dim), kv_mine, kv_mate)
        for c in chunks:
            s = dot_rows(q_rows[c, :], keys)
            for k in range(n):
                score[first + k, c, :] = s[:, k * keys_n : (k + 1) * keys_n]
            row_max[c, :] = functools.reduce(jnp.maximum, lane_tiles(s), row_max[c, :])

    by_pairs(count - 1, lambda first, n: score_blocks(first + 1, n))

    for c in chunks:
        top = jnp.max(row_max[c, :], axis=1, keepdims=True)
        row_max[c, :] = jnp.broadcast_to(top, (group, LANES))

    def weigh(first, n):
        values = stacked(order, first, n, slice(dim, 2 * dim), kv_mine, kv_mate)
        for c in chunks:
            top = row_max[c, :]
            blocks = [lane_tiles(score[first + k, c, :]) for k in range(n)]
            tiles = [[jnp.exp2(t - top) for t in b] for b in blocks]
            row_sum[c, :] += functools.reduce(jnp.add, sum(tiles, []))
            p = [jnp.concatenate(b, axis=1).astype(jnp.bfloat16) for b in tiles]
            for k in range(n):
                prob[first + k, c, :] = p[k]
            acc[c, :] += dot(jnp.concatenate(p, axis=1), values)

    by_pairs(count, weigh)

    lane = lax.broadcasted_iota(jnp.int32, (tok, LANES), 1)
    table = jnp.zeros((tok, LANES), jnp.float32)
    for j in range(2 * heads):
        r = slice(j * tok, (j + 1) * tok)
        grad = g_raw[r, :].astype(jnp.float32)
        columns = (row_max[r, :], lane_sum(row_sum[r, :]), lane_sum(grad * acc[r, :]))
        for k, column in enumerate(columns):
            table = jnp.where(lane == STAT_ROWS * k + j, column, table)
    stats[...] = jnp.transpose(table)[: stats.shape[0], :]


def backward(
    plan, prob, stats_own, stats_mate, acc_in, q_cols, g_raw, g_turned, kv_mine, kv_mate,
    out_keep, out_give, ds_out, dkv_keep, dkv_give,
    order, g_rows, ds_rows, delta_rows, g_cols, sems,
    *, tok, heads, dim, group,
):
    spans = order.shape[0]
    count, _ = visible_slots(plan, order, spans)

    half = heads * tok
    def parts_of(stats):
        return [stats[k * STAT_ROWS : (k + 1) * STAT_ROWS, :] for k in range(STATS)]

    def partner(x):
        return jnp.concatenate([x[heads : 2 * heads], x[:heads], x[2 * heads :]], axis=0)

    top_mine, sum_mine, delta_mine = parts_of(stats_own[...])
    top_other, sum_other, delta_other = [partner(x) for x in parts_of(stats_mate[...])]
    top = jnp.maximum(top_mine, top_other)
    f_mine, f_other = jnp.exp2(top_mine - top), jnp.exp2(top_other - top)
    total = sum_mine * f_mine + sum_other * f_other
    used = lax.broadcasted_iota(jnp.int32, total.shape, 0) < 2 * heads
    total = jnp.where(used, total, 1.0)
    scales = f_mine / total
    deltas = (delta_mine * f_mine + delta_other * f_other) / total * scales
    columns = columns_of(jnp.concatenate([scales, deltas], axis=0))
    for j in range(2 * heads):
        r = slice(j * tok, (j + 1) * tok)
        h = slice((j % heads) * dim, (j % heads + 1) * dim)
        scale = columns[:, j : j + 1]
        delta = columns[:, STAT_ROWS + j : STAT_ROWS + j + 1]
        delta_rows[r, :] = jnp.broadcast_to(delta, (tok, LANES))
        out = out_keep if j < heads else out_give
        g_rows[r, :] = (g_raw[r, :].astype(jnp.float32) * scale).astype(jnp.bfloat16)
        out[:, h] = (acc_in[r, :] * scale).astype(jnp.bfloat16)
    for j in range(2 * heads):
        r = slice(j * tok, (j + 1) * tok)
        turned = g_turned[:, r].astype(jnp.float32) * scales[j : j + 1, :]
        g_cols[:, r] = turned.astype(jnp.bfloat16)
    chunks = [slice(r, r + group) for r in range(0, 2 * half, group)]

    _, lower, own_span = unpack(plan, spans)

    @pl.loop(0, spans)
    def _(slot):
        span = plan[3 + 2 * spans + slot]

        @pl.when((span < lower) | (span > own_span))
        def _():
            dkv_keep[slot] = jnp.zeros(dkv_keep.shape[1:], dkv_keep.dtype)
            dkv_give[slot] = jnp.zeros(dkv_give.shape[1:], dkv_give.dtype)

    def grads_of(first, n):
        values = stacked(order, first, n, slice(dim, 2 * dim), kv_mine, kv_mate)
        for c in chunks:
            d_prob = lane_tiles(dot_rows(g_rows[c, :], values))
            delta = delta_rows[c, :]
            p = sum([lane_tiles(prob[first + k, c, :].astype(jnp.float32)) for k in range(n)], [])
            tiles = [x * (y - delta) for x, y in zip(p, d_prob)]
            per = len(tiles) // n
            for k in range(n):
                block = jnp.concatenate(tiles[k * per : (k + 1) * per], axis=1)
                ds_rows[first + k, c, :] = block.astype(jnp.bfloat16)
        for k in range(n):
            b = first + k
            pltpu.make_async_copy(ds_rows.at[b], ds_out.at[b], sems.at[b]).start()

    def keys_of(first, n):
        for k in range(n):
            slot = order[first + k]
            d_keys = jnp.transpose(dot(q_cols[...], ds_rows[first + k]) * LN2)
            d_keys = d_keys.astype(jnp.bfloat16)
            dkv_keep[slot, :, :dim] = d_keys[:tok]
            dkv_give[slot, :, :dim] = d_keys[tok:]
            d_values = jnp.transpose(dot(g_cols[...], prob[first + k])).astype(jnp.bfloat16)
            dkv_keep[slot, :, dim:] = d_values[:tok]
            dkv_give[slot, :, dim:] = d_values[tok:]

    by_pairs(count, grads_of)
    by_pairs(count, keys_of)

    @pl.loop(0, count)
    def _(b):
        pltpu.make_async_copy(ds_rows.at[b], ds_out.at[b], sems.at[b]).wait()


def finish(
    plan, ds_in, kv_mine, kv_mate, d_queries, order, ds_rows, acc, sems,
    *, tok, heads, dim, first_row,
):
    count, _ = visible_slots(plan, order, order.shape[0])
    n_rows = heads * tok

    def fetch(b):
        source = ds_in.at[b, pl.ds(first_row, n_rows)]
        return pltpu.make_async_copy(source, ds_rows.at[b], sems.at[b])

    @pl.loop(0, count)
    def _(b):
        fetch(b).start()

    acc[...] = jnp.zeros_like(acc)

    def add(first, n):
        keys = stacked(order, first, n, slice(0, dim), kv_mine, kv_mate)
        for k in range(n):
            fetch(first + k).wait()
        ds = jnp.concatenate([ds_rows[first + k] for k in range(n)], axis=1)
        acc[...] += dot(ds, keys)

    by_pairs(count, add)
    for h in range(heads):
        rows_of = acc[h * tok : (h + 1) * tok, :] / math.sqrt(dim)
        d_queries[:, h * dim : (h + 1) * dim] = rows_of.astype(jnp.bfloat16)


def spread(keys, values, queries, out, squares):
    both = jnp.concatenate([keys[...], values[...]], axis=1)
    for n in range(out.shape[0]):
        out[n] = both
    squares[...] = squares_of(queries[...])


SMEM_SPEC = pl.BlockSpec(memory_space=pltpu.SMEM)
HBM_SPEC = pl.BlockSpec(memory_space=pltpu.HBM)
VMEM_SPEC = pl.BlockSpec(memory_space=pltpu.VMEM)


def sizes_of(q_raw, kv_mine):
    n_rows, dim = q_raw.shape
    spans, tok, _ = kv_mine.shape
    return spans, tok, dim, n_rows // (2 * tok), n_rows


def small_params(limit=SMALL_LIMIT):
    return pltpu.CompilerParams(vmem_limit_bytes=limit)


def row_squares_call(own, q_mate):
    return pl.pallas_call(
        row_squares,
        out_shape=jax.ShapeDtypeStruct((2, own.shape[1]), jnp.float32),
        in_specs=[VMEM_SPEC] * 2,
        out_specs=VMEM_SPEC,
        compiler_params=small_params(),
        cost_estimate=LONG,
        name="row_squares",
    )(own, q_mate)


def normalize_call(square_sum, gain, q_raw, width):
    tok = square_sum.shape[1]
    n_rows, dim = q_raw.shape
    return pl.pallas_call(
        functools.partial(
            normalize, tok=tok, heads=n_rows // (2 * tok), dim=dim, width=width
        ),
        out_shape=(
            jax.ShapeDtypeStruct((n_rows, dim), jnp.bfloat16),
            jax.ShapeDtypeStruct((dim, n_rows), jnp.bfloat16),
        ),
        in_specs=[VMEM_SPEC] * 3,
        out_specs=(VMEM_SPEC,) * 2,
        compiler_params=small_params(),
        cost_estimate=SHORT,
        name="normalize",
    )(square_sum, gain, q_raw)


def prepare_call(queries, q_mate, out_grad, g_mate, dim):
    tok, local = queries.shape
    heads = local // dim
    rows = jax.ShapeDtypeStruct((2 * heads * tok, dim), jnp.bfloat16)
    return pl.pallas_call(
        functools.partial(prepare, tok=tok, heads=heads, dim=dim),
        out_shape=(rows, rows, jax.ShapeDtypeStruct((dim, 2 * heads * tok), jnp.bfloat16)),
        in_specs=[VMEM_SPEC] * 4,
        out_specs=(VMEM_SPEC,) * 3,
        compiler_params=small_params(),
        cost_estimate=SHORT,
        name="prepare",
    )(queries, q_mate, out_grad, g_mate)


def add_pair(one, other, out):
    out[...] = (one[...].astype(jnp.float32) + other[...].astype(jnp.float32)).astype(out.dtype)


def add_pair_call(one, other):
    return pl.pallas_call(
        add_pair,
        out_shape=jax.ShapeDtypeStruct(one.shape, jnp.bfloat16),
        in_specs=[VMEM_SPEC] * 2,
        out_specs=VMEM_SPEC,
        compiler_params=small_params(),
        name="add_pair",
    )(one, other)


def merge_call(*parts):
    rows = jax.ShapeDtypeStruct(parts[0].shape, jnp.bfloat16)
    return pl.pallas_call(
        merge,
        out_shape=(rows, rows),
        in_specs=[VMEM_SPEC] * 4,
        out_specs=(VMEM_SPEC,) * 2,
        compiler_params=small_params(),
        cost_estimate=SHORT,
        name="merge",
    )(*parts)


def forward_call(plan, q_rows, g_raw, kv_mine, kv_mate, group=384):
    spans, tok, dim, heads, n_rows = sizes_of(q_rows, kv_mine)
    return pl.pallas_call(
        functools.partial(forward, tok=tok, heads=heads, dim=dim, group=group),
        out_shape=(
            jax.ShapeDtypeStruct((spans, n_rows, 2 * tok), jnp.bfloat16),
            jax.ShapeDtypeStruct((n_rows, dim), jnp.float32),
            jax.ShapeDtypeStruct((STATS * STAT_ROWS, LANES), jnp.float32),
        ),
        in_specs=[SMEM_SPEC] + [VMEM_SPEC] * 4,
        out_specs=(VMEM_SPEC,) * 3,
        scratch_shapes=[
            pltpu.SMEM((spans,), jnp.int32),
            pltpu.VMEM((spans, n_rows, 2 * tok), jnp.float32),
            pltpu.VMEM((n_rows, LANES), jnp.float32),
            pltpu.VMEM((n_rows, LANES), jnp.float32),
        ],
        compiler_params=pltpu.CompilerParams(vmem_limit_bytes=VMEM_LIMIT),
        name="attend_forward",
    )(plan, q_rows, g_raw, kv_mine, kv_mate)


def backward_call(
    plan, prob, stats_own, stats_mate, acc, q_cols, g_raw, g_turned, kv_mine, kv_mate, group=768
):
    spans, tok, dim, heads, n_rows = sizes_of(g_raw, kv_mine)
    rows = jax.ShapeDtypeStruct((tok, heads * dim), jnp.bfloat16)
    part = jax.ShapeDtypeStruct(kv_mine.shape, jnp.bfloat16)
    return pl.pallas_call(
        functools.partial(backward, tok=tok, heads=heads, dim=dim, group=group),
        out_shape=(rows, rows, pltpu.HBM(prob.shape, jnp.bfloat16), part, part),
        in_specs=[SMEM_SPEC] + [VMEM_SPEC] * 9,
        out_specs=(VMEM_SPEC, VMEM_SPEC, HBM_SPEC, VMEM_SPEC, VMEM_SPEC),
        scratch_shapes=[
            pltpu.SMEM((spans,), jnp.int32),
            pltpu.VMEM((n_rows, dim), jnp.bfloat16),
            pltpu.VMEM(prob.shape, jnp.bfloat16),
            pltpu.VMEM((n_rows, LANES), jnp.float32),
            pltpu.VMEM((dim, n_rows), jnp.bfloat16),
            pltpu.SemaphoreType.DMA((spans,)),
        ],
        compiler_params=small_params(BACKWARD_LIMIT),
        name="attend_backward",
    )(plan, prob, stats_own, stats_mate, acc, q_cols, g_raw, g_turned, kv_mine, kv_mate)


def finish_call(plan, ds_rows, kv_mine, kv_mate, side, cost):
    ds_rows = pltpu.with_memory_space_constraint(ds_rows, pltpu.HBM)
    spans, n_rows, n_keys = ds_rows.shape
    _, tok, both = kv_mine.shape
    dim = both // 2
    half = n_rows // 2
    heads = half // tok
    return pl.pallas_call(
        functools.partial(finish, tok=tok, heads=heads, dim=dim, first_row=side * half),
        out_shape=jax.ShapeDtypeStruct((tok, heads * dim), jnp.bfloat16),
        in_specs=[SMEM_SPEC, HBM_SPEC, VMEM_SPEC, VMEM_SPEC],
        out_specs=VMEM_SPEC,
        scratch_shapes=[
            pltpu.SMEM((spans,), jnp.int32),
            pltpu.VMEM((spans, half, n_keys), jnp.bfloat16),
            pltpu.VMEM((half, dim), jnp.float32),
            pltpu.SemaphoreType.DMA((spans,)),
        ],
        compiler_params=small_params(),
        cost_estimate=cost,
        name=("finish_own", "finish_mate")[side],
    )(plan, ds_rows, kv_mine, kv_mate)


def spread_call(keys, values, queries, n_z):
    tok, dim = keys.shape
    return pl.pallas_call(
        spread,
        out_shape=(
            jax.ShapeDtypeStruct((n_z, tok, 2 * dim), jnp.bfloat16),
            jax.ShapeDtypeStruct((1, tok), jnp.float32),
        ),
        in_specs=[VMEM_SPEC] * 3,
        out_specs=(VMEM_SPEC,) * 2,
        name="spread",
    )(keys, values, queries)


def head_sum(x):
    x = x + lax.ppermute(x, "xl", SWAP)
    n = lax.axis_size("y")
    others = [lax.ppermute(x, "y", [(i, (i + d) % n) for i in range(n)]) for d in range(1, n)]
    return functools.reduce(jnp.add, others, x)


def shards(
    queries, key_states, value_states, out_grad, norm_gain, mask_kind, range_start, placement
):
    tok, local = queries.shape
    dim = key_states.shape[1]
    n_heads = lax.axis_size(HEAD)
    n_z = lax.axis_size("z")
    places = [lax.axis_index(a).astype(jnp.int32)[None] for a in CTX]
    plan = jnp.concatenate(places + [mask_kind, range_start, placement])

    q_mate = lax.ppermute(queries, "xh", SWAP)
    g_mate = lax.ppermute(out_grad, "xh", SWAP)
    kv_out, own_squares = spread_call(key_states, value_states, queries, n_z)
    kv_mine = lax.all_to_all(kv_out, "z", 0, 0)
    square_sum = head_sum(row_squares_call(own_squares, q_mate))
    q_raw, g_raw, g_turned = prepare_call(queries, q_mate, out_grad, g_mate, dim)
    kv_mine, square_sum, q_raw, g_raw = lax.optimization_barrier(
        (kv_mine, square_sum, q_raw, g_raw)
    )
    kv_mate = lax.ppermute(kv_mine, "core", SWAP)

    q_rows, q_cols = normalize_call(square_sum, norm_gain[None, :], q_raw, local * n_heads)
    prob, acc, stats = forward_call(plan, q_rows, g_raw, kv_mine, kv_mate)
    stats_mate = lax.ppermute(stats, "xh", SWAP)
    out_keep, out_give, ds_rows, dkv_keep, dkv_give = backward_call(
        plan, prob, stats, stats_mate, acc, q_cols, g_raw, g_turned, kv_mine, kv_mate
    )
    out_got = lax.ppermute(out_give, "xh", SWAP)
    dkv_got = lax.ppermute(dkv_give, "core", SWAP)
    chip = add_pair_call(dkv_keep, dkv_got)
    chip, ds_rows = lax.optimization_barrier((chip, ds_rows))
    pieces = lax.all_to_all(chip, "z", 0, 0)
    dq_give = finish_call(plan, ds_rows, kv_mine, kv_mate, 1, MEDIUM)
    dq_got = lax.ppermute(dq_give, "xh", SWAP)
    ds_rows, _ = lax.optimization_barrier((ds_rows, dq_give))
    dq_keep = finish_call(plan, ds_rows, kv_mine, kv_mate, 0, MEDIUM)
    attn_out, d_queries = merge_call(out_keep, out_got, dq_keep, dq_got)
    total = jnp.sum(pieces.astype(jnp.float32), axis=0).astype(jnp.bfloat16)
    return (attn_out, d_queries, total[:, :dim], total[:, dim:])


def solution(mesh):
    fine = Mesh(mesh.devices.reshape(8, 2, 2, 4, 2), ("z", "xh", "core", "y", "xl"))
    rows = P(CTX, HEAD)
    in_specs = (rows, rows, rows, rows, P(HEAD), P(), P(), P())
    out_specs = (rows, rows, rows, rows)
    return jax.shard_map(shards, mesh=fine, in_specs=in_specs, out_specs=out_specs, check_vma=False)
```
